32 devices in a mesh: row: 8 (over z, y), ga: 4 (over x, core).
Axes of the slice: x: 2, y: 2, z: 4, core: 2. Of those that a mesh axis runs over, the one named last changes fastest.
Arguments:
- fine_feats: bfloat16 [3584, 64, 512], P(('row', 'ga')), may hold values from -6 to 6
- fine_child: int32 [3584], P(('row', 'ga')), may hold values from -1 to 255, as said below
- parent_block: int32 [256], P(('row', 'ga')), may hold values from 0 to 63, as said below
- w_parent: bfloat16 [64, 128], replicated, may hold values from -2 to 2
- w_root_in: bfloat16 [128, 256], replicated, may hold values from -1.5 to 1.5
- w_root: bfloat16 [256, 256, 3, 3, 3], P('ga'), may hold values from -0.15625 to 0.15625
- root_bias: float32 [256], P('ga'), may hold values from -0.5 to 0.5
- w_down: bfloat16 [256, 128], replicated, may hold values from -0.375 to 0.375
- w_skip: bfloat16 [128, 64], replicated, may hold values from -0.5 to 0.5
Outputs:
- fine_out: bfloat16 [3584, 64, 512], P(('row', 'ga'))
- root_features: bfloat16 [256, 32, 32, 32], P('ga', 'row')
The draws below stay inside these ranges and needn't reach their ends.
Inputs may be any that keep to these rules, and one draw needn't show every extreme that they name: `fine_child`: parents i * 8 to (i + 1) * 8 - 1 of a region belong to the region's device of ga index i. Over the slots of a region every child index 0 to 255 appears exactly once. The slots of one device hold at most 28 children of one device's parents, and in every region some device holds exactly 28 children of each device's parents. `parent_block`: the parents of one region have distinct places.
All inputs are finite; a program needn't handle non-finite values.
Results may differ from the reference program's by a relative error of at most 0.013.
Values may be sent and summed in bfloat16 or wider, within the bound.
No kernel may reach another device: no remote copies, remote signals or barrier semaphores. Data moves between devices by JAX's collectives and lax.ppermute only.
A program may use at most 128 MiB of HBM per device.

```python
import jax
import jax.numpy as jnp
from jax import lax

C1 = 64
C2 = 128
C3 = 256
B = 8
PAR_DEV = 8
RXY = 32
RZ_REG = 4
PARENTS = 256
FINE_DEV = 112
FINE_SLOTS = 3584
RZ = 32
N_ROW = 8
N_GA = 4


def draw_region_children(region_key):
    groups = N_GA
    child_quota = 8 * PAR_DEV
    unit_load = child_quota // (groups * groups)
    split_keys = jax.random.split(region_key, 3)
    load_order = jax.random.permutation(split_keys[0], groups)
    send_loads = (2 * load_order + 1) * unit_load
    starts = jnp.cumsum(send_loads) - send_loads

    def shuffle_children(subkey):
        return jax.random.permutation(subkey, child_quota)

    def shuffle_slots(subkey):
        return jax.random.permutation(subkey, FINE_DEV)
    positions = jax.vmap(shuffle_children)(jax.random.split(split_keys[1], groups))
    sender = jnp.sum((positions[:, :, None] >= starts[None, None, :]).astype(jnp.int32), axis=2) - 1
    sender = sender.reshape(-1)
    sender_hot = (sender[:, None] == jnp.arange(groups, dtype=jnp.int32)[None, :]).astype(jnp.int32)
    slot_rank = jnp.sum(jnp.cumsum(sender_hot, axis=0) * sender_hot, axis=1) - 1
    slot_orders = jax.vmap(shuffle_slots)(jax.random.split(split_keys[2], groups))
    slot_place = slot_orders[sender, slot_rank]
    filled = jnp.full((groups, FINE_DEV), -1, jnp.int32)
    return filled.at[sender, slot_place].set(jnp.arange(groups * child_quota, dtype=jnp.int32))


def draw_fine_child(key, part):
    region_keys = jax.random.split(jax.random.fold_in(key, 11), N_ROW)
    return jax.vmap(draw_region_children)(region_keys).reshape(-1).astype(jnp.int32)


def draw_parent_block(key, part):
    half_edge = B // 2
    block_total = RZ_REG // half_edge * (RXY // half_edge) ** 2

    def region_places(subkey):
        return jax.random.permutation(subkey, block_total)[:N_GA * PAR_DEV]
    region_keys = jax.random.split(jax.random.fold_in(key, 23), N_ROW)
    return jax.vmap(region_places)(region_keys).reshape(-1).astype(jnp.int32)


def levels(key, dims, shards, low, largest):
    loudness, own = 1.0, jax.random.fold_in(key, 6)
    for axis_at, parts in shards:
        draws = jnp.exp(jax.random.uniform(jax.random.fold_in(own, axis_at), (parts,), jnp.float32, low / len(shards), largest / len(shards)))
        loudness = loudness * jnp.repeat(draws, dims[axis_at] // parts).reshape([-1 if axis == axis_at else 1 for axis in range(len(dims))])
    return loudness


def scatter_about(rng, shape, scale, limit, cuts=(), held_as=jnp.bfloat16):
    values = scale * jax.random.normal(rng, shape, jnp.float32)
    if cuts:
        values = values * levels(rng, shape, cuts, -0.22, 0.18)
    return jnp.clip(values, -limit, limit).astype(held_as)


def setup_inputs(seed: int = 0) -> dict:
    seeds = jax.random.split(jax.random.key(seed), 10)
    return {
        "fine_feats": scatter_about(seeds[0], (FINE_SLOTS, C1, B ** 3), 1.0, 6.0, ((0, 32),)),
        "fine_child": draw_fine_child(jax.random.fold_in(seeds[9], 71), 0),
        "parent_block": draw_parent_block(jax.random.fold_in(seeds[9], 71), 0),
        "w_parent": scatter_about(seeds[3], (C1, C2), (C1 // 8) ** -0.5, 2.0),
        "w_root_in": scatter_about(seeds[4], (C2, C3), (C2 // 8) ** -0.5, 1.5),
        "w_root": scatter_about(seeds[5], (C3, C3, 3, 3, 3), (27 * C3 // 4) ** -0.5, 0.15625, ((0, 4),)),
        "root_bias": jnp.clip(jax.random.uniform(seeds[6], (C3,), jnp.float32, -0.5, 0.5) * levels(seeds[6], (C3,), ((0, 4),), -0.4, 0.0), -0.5, 0.5),
        "w_down": scatter_about(seeds[7], (C3, C2), C3 ** -0.5, 0.375),
        "w_skip": scatter_about(seeds[8], (C2, C1), C2 ** -0.5, 0.5),
    }


def pool_pairs(values, half_edge):
    row_count, channel_count, voxel_count = values.shape
    cube = values.astype(jnp.float32).reshape(row_count, channel_count, half_edge, 2, half_edge, 2, half_edge, 2)
    return jnp.mean(cube, axis=(3, 5, 7)).reshape(row_count, channel_count, half_edge ** 3)


def upsample_pairs(values, half_edge):
    row_count, channel_count, voxel_count = values.shape
    cube = values.reshape(row_count, channel_count, half_edge, 1, half_edge, 1, half_edge, 1)
    cube = jnp.broadcast_to(cube, (row_count, channel_count, half_edge, 2, half_edge, 2, half_edge, 2))
    return cube.reshape(row_count, channel_count, 8 * voxel_count)


def join_octants(octants, half_edge):
    parent_count = octants.shape[0]
    channel_count = octants.shape[2]
    cube = octants.reshape(parent_count, 2, 2, 2, channel_count, half_edge, half_edge, half_edge)
    cube = cube.transpose(0, 4, 1, 5, 2, 6, 3, 7)
    return cube.reshape(parent_count, channel_count, 8 * half_edge ** 3)


def split_octants(bricks, half_edge):
    parent_count = bricks.shape[0]
    channel_count = bricks.shape[1]
    cube = bricks.reshape(parent_count, channel_count, 2, half_edge, 2, half_edge, 2, half_edge)
    cube = cube.transpose(0, 2, 4, 6, 1, 3, 5, 7)
    return cube.reshape(parent_count, 8, channel_count, half_edge ** 3)


def contract(values, weights):
    return jnp.einsum("pcv,cd->pdv", values.astype(jnp.float32), weights.astype(jnp.float32), precision=lax.Precision.HIGHEST)


def contract_octants(values, weights):
    return jnp.einsum("pocv,cd->podv", values.astype(jnp.float32), weights.astype(jnp.float32), precision=lax.Precision.HIGHEST)


def reference(fine_feats, fine_child, parent_block, w_parent, w_root_in, w_root, root_bias, w_down, w_skip):
    half_edge = B // 2
    octant_voxels = half_edge ** 3
    region_total = 8 * PAR_DEV * N_GA
    slot_region = (jnp.arange(FINE_SLOTS) // (FINE_DEV * N_GA)).astype(jnp.int32)
    live_slot = fine_child >= 0
    child_index = jnp.where(live_slot, slot_region * region_total + fine_child, 8 * PARENTS).astype(jnp.int32)
    pooled = pool_pairs(fine_feats, half_edge).astype(jnp.bfloat16)
    octant_table = jnp.zeros((8 * PARENTS + 1, C1, octant_voxels), jnp.bfloat16).at[child_index].set(pooled)[:-1]
    bricks = join_octants(octant_table.reshape(PARENTS, 8, C1, octant_voxels), half_edge)
    parent_hidden = jax.nn.relu(contract(bricks, w_parent)).astype(jnp.bfloat16)
    parent_pool = pool_pairs(parent_hidden, half_edge).astype(jnp.bfloat16)
    root_input = contract(parent_pool, w_root_in).astype(jnp.bfloat16)
    block_side = RXY // half_edge
    block_layers = RZ_REG // half_edge
    block_total = block_layers * block_side * block_side
    parent_region = (jnp.arange(PARENTS) // (PAR_DEV * N_GA)).astype(jnp.int32)
    block_index = (parent_region * block_total + parent_block).astype(jnp.int32)
    placed = jnp.zeros((N_ROW * block_total, C3, octant_voxels), jnp.bfloat16).at[block_index].set(root_input)
    root_grid = placed.reshape(N_ROW, block_layers, block_side, block_side, C3, half_edge, half_edge, half_edge)
    root_grid = root_grid.transpose(4, 0, 1, 5, 2, 6, 3, 7).reshape(C3, RZ, RXY, RXY)
    convolved = lax.conv_general_dilated(root_grid[None].astype(jnp.float32), w_root.astype(jnp.float32), (1, 1, 1), ((1, 1), (1, 1), (1, 1)), dimension_numbers=("NCDHW", "OIDHW", "NCDHW"), precision=lax.Precision.HIGHEST)[0]
    root_features = jax.nn.relu(convolved + root_bias[:, None, None, None]).astype(jnp.bfloat16)
    blocks_back = root_features.reshape(C3, N_ROW, block_layers, half_edge, block_side, half_edge, block_side, half_edge)
    blocks_back = blocks_back.transpose(1, 2, 4, 6, 0, 3, 5, 7).reshape(N_ROW * block_total, C3, octant_voxels)
    parent_root = blocks_back[block_index]
    lifted = contract(parent_root, w_down)
    parent_decoded = jax.nn.relu(parent_hidden.astype(jnp.float32) + upsample_pairs(lifted, half_edge)).astype(jnp.bfloat16)
    skip_octants = contract_octants(split_octants(parent_decoded, half_edge), w_skip).astype(jnp.bfloat16)
    skip_octants = skip_octants.reshape(8 * PARENTS, C1, octant_voxels)
    fine_skip = jnp.where(live_slot[:, None, None], skip_octants[jnp.minimum(child_index, 8 * PARENTS - 1)], 0).astype(jnp.float32)
    fine_out = (fine_feats.astype(jnp.float32) + upsample_pairs(fine_skip, half_edge)).astype(jnp.bfloat16)
    return fine_out, root_features
```

```python
import functools

import jax
import jax.numpy as jnp
from jax import lax
from jax.experimental import pallas as pl
from jax.experimental.pallas import tpu as pltpu
from jax.sharding import PartitionSpec as P

B = 8
RXY = 32
RZ_REG = 4

HALF = B // 2
OCT = RXY // 2
LAYERS = RZ_REG // 2
PLANE = OCT * OCT
BORDERED = PLANE + 2 * OCT
SUBS = 8
META = 16
BF16 = jnp.bfloat16
F32 = jnp.float32
VMEM = pl.BlockSpec(memory_space=pltpu.VMEM)
SMEM = pl.BlockSpec(memory_space=pltpu.SMEM)


def params(mib):
    return pltpu.CompilerParams(vmem_limit_bytes=mib << 20)


def cost(macs, moved):
    return pl.CostEstimate(flops=2 * macs, bytes_accessed=moved, transcendentals=0)


def iota(shape, axis):
    return lax.broadcasted_iota(jnp.int32, shape, axis)


def dot(left, right):
    return jnp.dot(left, right, preferred_element_type=F32)


def dot_nt(left, right):
    return lax.dot_general(left, right, (((1,), (1,)), ((), ())), preferred_element_type=F32)


def hidden_voxel(fine):
    z, y, x = fine // (B * B), fine // B % B, fine % B
    low = z // 2 % 2 * 4 + y // 2 % 2 * 2 + x // 2 % 2
    high = z // HALF * 4 + y // HALF * 2 + x // HALF
    return low * SUBS + high


def fine_in_kernel(
    child_ref, block_ref, fine_ref, w_ref, hidden_ref, pooled_ref, pool, weights, tops, meta, *, total, padded
):
    step = pl.program_id(0)
    chunk, width, voxels = fine_ref.shape
    depth = w_ref.shape[1]
    group = hidden_ref.shape[2] // depth
    cells = voxels // SUBS

    @pl.when(step == 0)
    def _():
        hit = hidden_voxel(iota((voxels, cells), 0)) == iota((voxels, cells), 1)
        pool[...] = jnp.where(hit, 1.0 / SUBS, 0.0).astype(BF16)
        weights[...] = jnp.zeros_like(weights)
        for s in range(group):
            weights[s * width : (s + 1) * width, s * depth : (s + 1) * depth] = w_ref[...]
        meta[...] = jnp.full_like(meta, -1.0)
        meta[0:1, 0:total] = (child_ref[...] >> 3).astype(F32)
        meta[1:2, 0:total] = (child_ref[...] & 7).astype(F32)
        meta[2:3, 0 : block_ref.shape[1]] = block_ref[...].astype(F32)
        pooled_ref[SUBS * padded : SUBS * padded + META, :] = meta[...].astype(BF16)

    for j in range(chunk // group):
        cube = fine_ref[j * group : (j + 1) * group].reshape(group * width, voxels)
        octants = dot(cube, pool[...]).astype(BF16)
        hidden = jnp.maximum(dot(octants.T, weights[...]), 0.0).astype(BF16)
        hidden_ref[j] = hidden
        top = jnp.sum(hidden.astype(F32).reshape(SUBS, SUBS, group * depth), axis=0) * (1.0 / SUBS)
        for s in range(group):
            at = (j * group + s) * SUBS
            tops[at : at + SUBS, :] = top[:, s * depth : (s + 1) * depth]
    if padded != total:
        slot = step * chunk + iota(tops.shape, 0) // SUBS
        tops[...] = jnp.where(slot < total, tops[...], 0.0)
    for v in range(SUBS):
        at = pl.multiple_of(v * padded + step * chunk, chunk)
        pooled_ref[pl.ds(at, chunk), :] = tops[pl.ds(v, chunk, stride=SUBS), :].astype(BF16)


def fine_in(fine_feats, fine_child, parent_block, w_parent, chunk, padded):
    total, width, voxels = fine_feats.shape
    depth = w_parent.shape[1]
    group = 256 // width
    cells = voxels // SUBS
    return pl.pallas_call(
        functools.partial(fine_in_kernel, total=total, padded=padded),
        grid=(padded // chunk,),
        in_specs=[
            pl.BlockSpec((1, total), lambda i: (0, 0)),
            pl.BlockSpec((1, parent_block.shape[0]), lambda i: (0, 0)),
            pl.BlockSpec((chunk, width, voxels), lambda i: (i, 0, 0)),
            pl.BlockSpec((width, depth), lambda i: (0, 0)),
        ],
        out_specs=[
            pl.BlockSpec((chunk // group, cells, group * depth), lambda i: (i, 0, 0)),
            pl.BlockSpec((SUBS * padded + META, depth), lambda i: (0, 0)),
        ],
        out_shape=[
            jax.ShapeDtypeStruct((padded // group, cells, group * depth), BF16),
            jax.ShapeDtypeStruct((SUBS * padded + META, depth), BF16),
        ],
        scratch_shapes=[
            pltpu.VMEM((voxels, cells), BF16),
            pltpu.VMEM((group * width, group * depth), BF16),
            pltpu.VMEM((chunk * SUBS, depth), F32),
            pltpu.VMEM((META, 128), F32),
        ],
        compiler_params=params(24),
        cost_estimate=cost(total * width * voxels * 256, 2 * total * width * voxels),
        name="fine_in",
    )(fine_child[None], parent_block[None], fine_feats, w_parent)


def fold_kernel(w_ref, in_ref, out_ref):
    share = w_ref.shape[3]
    depth = in_ref.shape[0]
    nothing = jnp.zeros((share, w_ref.shape[4]), BF16)
    out_ref[:, 0, :, 2 * share :] = jnp.zeros((3, 4 * depth, 2 * share), BF16)
    out_ref[:, 3, :, 0 : 2 * share] = jnp.zeros((3, 4 * depth, 2 * share), BF16)
    for a in range(3):
        for b in range(3):
            for j in range(4):
                first = w_ref[a, b, j] if j < 3 else nothing
                second = w_ref[a, b, j - 1] if j > 0 else nothing
                pair = jnp.concatenate([first, second], axis=0)
                folded = dot_nt(in_ref[...], pair).astype(BF16)
                rows = slice(j * depth, (j + 1) * depth)
                out_ref[a, b, rows, 0 : 2 * share] = folded
                out_ref[a, b + 1, rows, 2 * share : 4 * share] = folded


def fold(w_root, w_root_in):
    share = w_root.shape[0]
    depth = w_root_in.shape[0]
    return pl.pallas_call(
        fold_kernel,
        in_specs=[VMEM, VMEM],
        out_specs=VMEM,
        out_shape=jax.ShapeDtypeStruct((3, 4, 4 * depth, 4 * share), BF16),
        compiler_params=params(16),
        cost_estimate=cost(36 * depth * 256 * 128, 6 << 20),
        name="fold",
    )(w_root.transpose(2, 3, 4, 0, 1), w_root_in)


def y_window(j):
    return ((1, 0), (0, OCT), (1, OCT), (0, 2 * OCT))[j]


def place_kernel(offsets, padded, pairs, *refs):
    groups = len(offsets)
    pooled_refs, w_ref = refs[:groups], refs[groups]
    grid_ref, place_ref, pair_ref, step_ref = refs[groups + 1 : groups + 5]
    table = refs[groups + 5]
    depth = pooled_refs[0].shape[1]
    lane_count = groups * 128
    me = lax.axis_index("ga")
    row = lax.axis_index("row")

    metas = [r[SUBS * padded : SUBS * padded + META, :] for r in pooled_refs]
    parent = jnp.concatenate([m[0:1].astype(F32) for m in metas], axis=1).astype(jnp.int32)
    octant = jnp.concatenate([m[1:2].astype(F32) for m in metas], axis=1).astype(jnp.int32)
    found = jnp.zeros((META, lane_count), F32)
    for k, offset in enumerate(offsets):
        at = iota((128, lane_count), 0)
        hot = (at < pairs) & (parent == at + (me ^ offset) * pairs)
        found += dot(metas[k], jnp.where(hot, 1.0, 0.0).astype(BF16))
    block = found[2:3].astype(jnp.int32)
    side = RXY // HALF
    z = block // (side * side) * 2 + (octant >> 2)
    y = block // side % side * 2 + (octant >> 1) % 2
    x = block % side * 2 + octant % 2
    live = parent >= 0
    place = jnp.where(live, (z * OCT + y) * OCT + x, -1)
    place_ref[...] = jnp.broadcast_to(place, place_ref.shape)

    for k, pooled_ref in enumerate(pooled_refs):
        for v in range(SUBS):
            vz, vy, vx = v >> 2, v >> 1 & 1, v & 1
            lanes = slice((vx * 4 + vz * 2 + vy) * depth, (vx * 4 + vz * 2 + vy + 1) * depth)
            table[k * 128 : k * 128 + padded, lanes] = pooled_ref[v * padded : (v + 1) * padded, :]
            if padded < 128:
                table[k * 128 + padded : (k + 1) * 128, lanes] = jnp.zeros((128 - padded, depth), BF16)

    grid_ref[:, :, 0:OCT, :] = jnp.zeros((2, RZ_REG, OCT, 4 * depth), BF16)
    grid_ref[:, :, OCT + PLANE :, :] = jnp.zeros((2, RZ_REG, OCT, 4 * depth), BF16)
    shifted = (
        (0, 1, jnp.where(live & (x < OCT - 1), place + 1, -1)),
        (1, 0, place),
        (2, 1, place),
        (3, 0, jnp.where(live & (x > 0), place - 1, -1)),
    )
    for j, vx, at in shifted:
        hot = jnp.where(iota((LAYERS * PLANE, lane_count), 0) == at, 1.0, 0.0).astype(BF16)
        for vz in range(2):
            first = (vx * 4 + vz * 2) * depth
            both = dot(hot, table[:, first : first + 2 * depth]).astype(BF16)
            for vy in range(2):
                for layer in range(LAYERS):
                    grid_ref[vy, layer * 2 + vz, OCT : OCT + PLANE, j * depth : (j + 1) * depth] = both[
                        layer * PLANE : (layer + 1) * PLANE, vy * depth : (vy + 1) * depth
                    ]

    even = row % 2 == 0
    for out_ref, up in ((pair_ref, even), (step_ref, jnp.logical_not(even))):
        plane = jnp.where(up, RZ_REG - 1, 0)
        dz = jnp.where(up, 0, 2)
        total = None
        for j in range(4):
            vy, first = y_window(j)
            part = dot(grid_ref[vy, plane, first : first + PLANE, :], w_ref[dz, j])
            total = part if total is None else total + part
        out_ref[...] = total.astype(BF16)


def place(pooled, offsets, folded, padded, pairs):
    groups = len(offsets)
    depth = pooled[0].shape[1]
    wide = folded.shape[3]
    return pl.pallas_call(
        functools.partial(place_kernel, offsets, padded, pairs),
        in_specs=[VMEM] * (groups + 1),
        out_specs=[VMEM] * 4,
        out_shape=[
            jax.ShapeDtypeStruct((2, RZ_REG, BORDERED, 4 * depth), BF16),
            jax.ShapeDtypeStruct((8, groups * 128), jnp.int32),
            jax.ShapeDtypeStruct((PLANE, wide), BF16),
            jax.ShapeDtypeStruct((PLANE, wide), BF16),
        ],
        scratch_shapes=[pltpu.VMEM((groups * 128, SUBS * depth), BF16)],
        compiler_params=params(24),
        cost_estimate=cost(2 << 28, 6 << 20),
        name="place",
    )(*pooled, folded)


def conv_kernel(grid_ref, w_ref, out_ref):
    for z in range(RZ_REG):
        total = None
        for a in range(3):
            if not 0 <= z + a - 1 < RZ_REG:
                continue
            for j in range(4):
                vy, first = y_window(j)
                part = dot(grid_ref[vy, z + a - 1, first : first + PLANE, :], w_ref[a, j])
                total = part if total is None else total + part
        out_ref[z] = total


def conv(grid, folded):
    wide = folded.shape[3]
    return pl.pallas_call(
        conv_kernel,
        in_specs=[VMEM, VMEM],
        out_specs=VMEM,
        out_shape=jax.ShapeDtypeStruct((RZ_REG, PLANE, wide), F32),
        compiler_params=params(16),
        cost_estimate=cost(10 * 4 * PLANE * 512 * 256, 6 << 20),
        name="conv",
    )(grid, folded)


def finish_kernel(padded, place_ref, sums_ref, pair_ref, step_ref, bias_ref, *refs):
    groups = len(refs) - 1
    root_ref, send_refs = refs[0], refs[1:]
    lane_count = place_ref.shape[1]
    row = lax.axis_index("row")
    even = row % 2 == 0
    has_pair_up = even
    last = lax.axis_size("row") - 1
    bias = jnp.concatenate([bias_ref[...]] * 4, axis=1)
    pair = pair_ref[...].astype(F32)
    step = step_ref[...].astype(F32)
    above = jnp.where(even, pair, step)
    below = jnp.where(even, step, pair)
    above = jnp.where(row < last, above, 0.0)
    below = jnp.where(row > 0, below, 0.0)
    del has_pair_up
    column = place_ref[...].astype(F32).T[:, 0:1].astype(jnp.int32)
    hot = jnp.where(column == iota((lane_count, LAYERS * PLANE), 1), 1.0, 0.0).astype(BF16)
    for z in range(RZ_REG):
        total = sums_ref[z] + bias
        if z == 0:
            total += below
        if z == RZ_REG - 1:
            total += above
        root_ref[z % 2, z // 2 * PLANE : (z // 2 + 1) * PLANE, :] = jnp.maximum(total, 0.0).astype(BF16)
    wide = root_ref.shape[2]
    for vz in range(2):
        picked = dot(hot, root_ref[vz]).astype(BF16)
        for k in range(groups):
            send_refs[k][:, vz * wide : (vz + 1) * wide] = picked[k * 128 : k * 128 + padded]


def finish(places, sums, pair, step, root_bias, groups, padded):
    wide = sums.shape[2]
    return pl.pallas_call(
        functools.partial(finish_kernel, padded),
        in_specs=[VMEM] * 5,
        out_specs=[VMEM] * (groups + 1),
        out_shape=[jax.ShapeDtypeStruct((2, LAYERS * PLANE, wide), BF16)]
        + [jax.ShapeDtypeStruct((padded, 2 * wide), BF16)] * groups,
        compiler_params=params(24),
        cost_estimate=cost(1 << 27, 3 << 20),
        name="finish",
    )(places, sums, pair, step, root_bias[None])


def unravel_kernel(root_ref, out_ref):
    share = root_ref.shape[2] // 4
    rows, half = 2 * PLANE // 2, PLANE // 2
    x, y = iota((rows, half), 0), iota((rows, half), 1)
    same = x // RXY == y // OCT
    spread = [
        jnp.where(same & (x % RXY == 2 * (y % OCT) + vx), 1.0, 0.0).astype(BF16) for vx in range(2)
    ]
    lines = half // OCT
    for z in range(RZ_REG):
        for part in range(2):
            first = z // 2 * PLANE + part * half
            for vy in range(2):
                at = vy * 2 * share
                even = root_ref[z % 2, first : first + half, at : at + share]
                odd = root_ref[z % 2, first : first + half, at + share : at + 2 * share]
                line = (dot(spread[0], even) + dot(spread[1], odd)).astype(BF16)
                out_ref[z, part * lines : (part + 1) * lines, vy] = line.reshape(lines, RXY, share)


def unravel(root):
    share = root.shape[2] // 4
    out = pl.pallas_call(
        unravel_kernel,
        in_specs=[VMEM],
        out_specs=VMEM,
        out_shape=jax.ShapeDtypeStruct((RZ_REG, OCT, 2, RXY, share), BF16),
        compiler_params=params(16),
        cost_estimate=cost(1 << 28, 2 << 20),
        name="unravel",
    )(root)
    return out.reshape(RZ_REG, RXY, RXY, share).transpose(3, 0, 1, 2)


def fine_out_kernel(offsets, *refs):
    groups = len(offsets)
    child_ref, fine_ref, hidden_ref, down_ref, skip_ref = refs[:5]
    come_refs = refs[5 : 5 + groups]
    out_ref = refs[5 + groups]
    spread, weights, down, lifted = refs[6 + groups :]
    step = pl.program_id(0)
    chunk, width, voxels = fine_ref.shape
    depth = down_ref.shape[1]
    group = hidden_ref.shape[2] // depth
    cells = voxels // SUBS
    total = child_ref.shape[0]
    share = come_refs[0].shape[1] // SUBS
    me = lax.axis_index("ga")

    @pl.when(step == 0)
    def _():
        hit = hidden_voxel(iota((cells, voxels), 1)) == iota((cells, voxels), 0)
        spread[...] = jnp.where(hit, 1.0, 0.0).astype(BF16)
        weights[...] = jnp.zeros_like(weights)
        turned = skip_ref[...].T
        for s in range(group):
            weights[s * depth : (s + 1) * depth, s * width : (s + 1) * width] = turned
        down[...] = jnp.zeros_like(down)
        for k, offset in enumerate(offsets):
            rows = down_ref[pl.ds(pl.multiple_of((me ^ offset) * share, share), share), :]
            for vx in range(2):
                first = (k * 2 + vx) * share
                down[first : first + share, vx * depth : (vx + 1) * depth] = rows
        for zy in range(4):
            lanes = slice(zy * 2 * share, (zy + 1) * 2 * share)
            both = dot(jnp.concatenate([r[:, lanes] for r in come_refs], axis=1), down[...])
            slots = both.shape[0]
            for vx in range(2):
                lifted[pl.ds(zy * 2 + vx, slots, stride=SUBS), :] = both[:, vx * depth : (vx + 1) * depth]

    for j in range(chunk // group):
        parts = []
        for s in range(group):
            slot = step * chunk + j * group + s
            hidden = hidden_ref[j, :, s * depth : (s + 1) * depth].astype(F32)
            top = lifted[pl.ds(pl.multiple_of(slot * SUBS, SUBS), SUBS), :]
            both = jnp.maximum(hidden.reshape(SUBS, SUBS, depth) + top[None], 0.0)
            live = child_ref[jnp.minimum(slot, total - 1)] >= 0
            parts.append(jnp.where(live, both, 0.0).reshape(cells, depth).astype(BF16))
        skip = dot(jnp.concatenate(parts, axis=1), weights[...]).astype(BF16)
        up = dot(skip.T, spread[...])
        cube = fine_ref[j * group : (j + 1) * group].reshape(group * width, voxels)
        out = (cube.astype(F32) + up).astype(BF16)
        out_ref[j * group : (j + 1) * group] = out.reshape(group, width, voxels)


def fine_out(fine_feats, fine_child, hidden, w_down, w_skip, come, offsets, chunk, padded):
    total, width, voxels = fine_feats.shape
    depth = w_down.shape[1]
    group = 256 // width
    cells = voxels // SUBS
    groups = len(offsets)
    share = come[0].shape[1] // SUBS

    def whole(array):
        return pl.BlockSpec(array.shape, lambda i: (0,) * array.ndim)

    turned = w_skip.T
    return pl.pallas_call(
        functools.partial(fine_out_kernel, offsets),
        grid=(padded // chunk,),
        in_specs=[
            SMEM,
            pl.BlockSpec((chunk, width, voxels), lambda i: (i, 0, 0)),
            pl.BlockSpec((chunk // group, cells, group * depth), lambda i: (i, 0, 0)),
            whole(w_down),
            whole(turned),
        ]
        + [whole(c) for c in come],
        out_specs=pl.BlockSpec((chunk, width, voxels), lambda i: (i, 0, 0)),
        out_shape=jax.ShapeDtypeStruct(fine_feats.shape, BF16),
        scratch_shapes=[
            pltpu.VMEM((cells, voxels), BF16),
            pltpu.VMEM((group * depth, group * width), BF16),
            pltpu.VMEM((groups * 2 * share, 2 * depth), BF16),
            pltpu.VMEM((padded * SUBS, depth), F32),
        ],
        compiler_params=params(24),
        cost_estimate=cost(total * width * voxels * 256, 4 * total * width * voxels),
        name="fine_out",
    )(fine_child, fine_feats, hidden, w_down, turned, *come)


def shards(
    fine_feats, fine_child, parent_block, w_parent, w_root_in, w_root, root_bias, w_down, w_skip
):
    groups = lax.axis_size("ga")
    rows = lax.axis_size("row")
    slots = fine_feats.shape[0]
    chunk = 16
    padded = -(-slots // chunk) * chunk
    pairs = parent_block.shape[0]

    hidden, pooled = fine_in(fine_feats, fine_child, parent_block, w_parent, chunk, padded)

    gathered, offsets = [pooled], [0]
    bit = groups // 2
    while bit:
        swap = [(i, i ^ bit) for i in range(groups)]
        gathered += [lax.ppermute(part, "ga", swap) for part in gathered]
        offsets += [offset ^ bit for offset in offsets]
        bit //= 2
    offsets = tuple(offsets)

    folded = fold(w_root, w_root_in)
    grid, places, pair, step = place(gathered, offsets, folded, padded, pairs)
    pair_swap = [(i, i ^ 1) for i in range(rows) if i ^ 1 < rows]
    step_swap = [(i, (i - 1 ^ 1) + 1) for i in range(1, rows) if (i - 1 ^ 1) + 1 < rows]
    pair = lax.ppermute(pair, "row", pair_swap)
    step = lax.ppermute(step, "row", step_swap)
    sums = conv(grid, folded)
    root, *sends = finish(places, sums, pair, step, root_bias, groups, padded)
    come = [sends[0]]
    for offset, send in zip(offsets[1:], sends[1:]):
        come.append(lax.ppermute(send, "ga", [(i, i ^ offset) for i in range(groups)]))
    root_out = unravel(root)
    fine = fine_out(fine_feats, fine_child, hidden, w_down, w_skip, come, offsets, chunk, padded)
    return (fine, root_out)


def solution(mesh):
    return jax.shard_map(
        shards,
        mesh=mesh,
        in_specs=(
            P(("row", "ga"), None, None),
            P(("row", "ga")),
            P(("row", "ga")),
            P(),
            P(),
            P("ga", None, None, None, None),
            P("ga"),
            P(),
            P(),
        ),
        out_specs=(P(("row", "ga"), None, None), P("ga", "row", None, None)),
        check_vma=False,
    )
```

```python
import functools

import jax
import jax.numpy as jnp
from jax import lax
from jax.experimental import pallas as pl
from jax.experimental.pallas import tpu as pltpu
from jax.sharding import PartitionSpec as P

B = 8
RXY = 32
RZ_REG = 4

HALF = B // 2
OCT = RXY // 2
LAYERS = RZ_REG // 2
PLANE = OCT * OCT
BORDERED = PLANE + 2 * OCT
SUBS = 8
AHEAD = 2
META = 16
BF16 = jnp.bfloat16
F32 = jnp.float32
VMEM = pl.BlockSpec(memory_space=pltpu.VMEM)
ANY = pl.BlockSpec(memory_space=pl.ANY)


def params(mib):
    return pltpu.CompilerParams(vmem_limit_bytes=mib << 20)


def cost(macs, moved):
    return pl.CostEstimate(flops=2 * macs, bytes_accessed=moved, transcendentals=0)


def iota(shape, axis):
    return lax.broadcasted_iota(jnp.int32, shape, axis)


def dot(left, right):
    return jnp.dot(left, right, preferred_element_type=F32)


def dot_nt(left, right):
    return lax.dot_general(left, right, (((1,), (1,)), ((), ())), preferred_element_type=F32)


def hidden_voxel(fine):
    edge = B.bit_length() - 1
    z, y, x = fine >> 2 * edge, fine >> edge & B - 1, fine & B - 1
    low = (z >> 1 & 1) * 4 + (y >> 1 & 1) * 2 + (x >> 1 & 1)
    high = (z >> edge - 1) * 4 + (y >> edge - 1) * 2 + (x >> edge - 1)
    return low * SUBS + high


def parts_of(total, group, most):
    return max(n for n in range(group, most + 1, group) if total % n == 0)


def fine_in_kernel(
    child_hbm, block_hbm, fine_hbm, w_hbm, hidden_hbm, pooled_ref, fine_ref, hidden_ref,
    child_ref, block_ref, w_ref, pool, weights, turned, tops, meta, fine_sems, hidden_sems, sems, *, total, padded
):
    _, width, voxels = fine_ref.shape
    depth = w_ref.shape[1]
    group = hidden_ref.shape[2] // depth
    cells = voxels // SUBS
    chunk = total // fine_sems.shape[0]
    sets = chunk // group

    def fetch(i):
        part = pl.ds(i * chunk, chunk)
        return pltpu.make_async_copy(fine_hbm.at[part], fine_ref.at[part], fine_sems.at[i])

    def store(i):
        part = pl.ds(i * sets, sets)
        return pltpu.make_async_copy(hidden_ref.at[part], hidden_hbm.at[part], hidden_sems.at[i])

    fetch(0).start()
    small = [
        pltpu.make_async_copy(source, target, sems.at[i])
        for i, (source, target) in enumerate(
            ((w_hbm, w_ref), (child_hbm, child_ref), (block_hbm, block_ref))
        )
    ]
    for copy in small:
        copy.start()
    for i in range(1, min(AHEAD, total // chunk)):
        fetch(i).start()

    hit = hidden_voxel(iota((voxels, cells), 0)) == iota((voxels, cells), 1)
    pool[...] = jnp.where(hit, 1.0 / SUBS, 0.0).astype(BF16)
    weights[...] = jnp.zeros_like(weights)
    for copy in small:
        copy.wait()
    for s in range(group):
        weights[s * width : (s + 1) * width, s * depth : (s + 1) * depth] = w_ref[...]
    meta[...] = jnp.full_like(meta, -1.0)
    meta[0:1, 0:total] = (child_ref[...] >> 3).astype(F32)
    meta[1:2, 0:total] = (child_ref[...] & 7).astype(F32)
    meta[2:3, 0 : block_ref.shape[1]] = block_ref[...].astype(F32)
    pooled_ref[SUBS * padded : SUBS * padded + META, :] = meta[...].astype(BF16)

    for i in range(total // chunk):
        fetch(i).wait()
        if i + AHEAD < total // chunk:
            fetch(i + AHEAD).start()
        cube = fine_ref[i * chunk : (i + 1) * chunk].reshape(chunk * width, voxels)
        octants = dot(cube, pool[...]).astype(BF16)
        for g in range(sets):
            at = (i * sets + g) * cells
            turned[at : at + cells, :] = octants[g * group * width : (g + 1) * group * width].T
    for i in range(total // chunk):
        rows = turned[i * sets * cells : (i + 1) * sets * cells, :]
        hidden = jnp.maximum(dot(rows, weights[...]), 0.0).astype(BF16)
        hidden_ref[i * sets : (i + 1) * sets] = hidden.reshape(sets, cells, group * depth)
        store(i).start()
        cubes = hidden.astype(F32).reshape(sets, SUBS, SUBS, group * depth)
        top = jnp.sum(cubes, axis=1) * (1.0 / SUBS)
        for g in range(sets):
            for s in range(group):
                at = (i * chunk + g * group + s) * SUBS
                tops[at : at + SUBS, :] = top[g, :, s * depth : (s + 1) * depth]
    if padded != total:
        tops[total * SUBS :, :] = jnp.zeros(((padded - total) * SUBS, depth), F32)
    for v in range(SUBS):
        pooled_ref[v * padded : (v + 1) * padded, :] = tops[pl.ds(v, padded, stride=SUBS), :].astype(BF16)
    for i in range(total // chunk):
        store(i).wait()


def fine_in(fine_feats, fine_child, parent_block, w_parent, padded):
    total, width, voxels = fine_feats.shape
    depth = w_parent.shape[1]
    pairs = parent_block.shape[0]
    group = 256 // width
    cells = voxels // SUBS
    chunk = parts_of(total, group, 16)
    return pl.pallas_call(
        functools.partial(fine_in_kernel, total=total, padded=padded),
        in_specs=[ANY] * 4,
        out_specs=[ANY, VMEM],
        out_shape=[
            jax.ShapeDtypeStruct((total // group, cells, group * depth), BF16),
            jax.ShapeDtypeStruct((SUBS * padded + META, depth), BF16),
        ],
        scratch_shapes=[
            pltpu.VMEM(fine_feats.shape, BF16),
            pltpu.VMEM((total // group, cells, group * depth), BF16),
            pltpu.VMEM((1, total), jnp.int32),
            pltpu.VMEM((1, pairs), jnp.int32),
            pltpu.VMEM(w_parent.shape, BF16),
            pltpu.VMEM((voxels, cells), BF16),
            pltpu.VMEM((group * width, group * depth), BF16),
            pltpu.VMEM((total // group * cells, group * width), BF16),
            pltpu.VMEM((padded * SUBS, depth), F32),
            pltpu.VMEM((META, 128), F32),
            pltpu.SemaphoreType.DMA((total // chunk,)),
            pltpu.SemaphoreType.DMA((total // chunk,)),
            pltpu.SemaphoreType.DMA((3,)),
        ],
        compiler_params=params(58),
        cost_estimate=cost(total * width * voxels * 256, 2 * total * width * voxels),
        name="fine_in",
    )(fine_child[None], parent_block[None], fine_feats, w_parent)


def fold_kernel(w_ref, in_ref, out_ref):
    share = w_ref.shape[3]
    depth = in_ref.shape[0]
    nothing = jnp.zeros((share, w_ref.shape[4]), BF16)
    out_ref[:, 0, :, 2 * share :] = jnp.zeros((3, 4 * depth, 2 * share), BF16)
    out_ref[:, 3, :, 0 : 2 * share] = jnp.zeros((3, 4 * depth, 2 * share), BF16)
    for a in range(3):
        for b in range(3):
            for j in range(4):
                first = w_ref[a, b, j] if j < 3 else nothing
                second = w_ref[a, b, j - 1] if j > 0 else nothing
                pair = jnp.concatenate([first, second], axis=0)
                folded = dot_nt(in_ref[...], pair).astype(BF16)
                rows = slice(j * depth, (j + 1) * depth)
                out_ref[a, b, rows, 0 : 2 * share] = folded
                out_ref[a, b + 1, rows, 2 * share : 4 * share] = folded


def fold(w_root, w_root_in):
    share = w_root.shape[0]
    depth = w_root_in.shape[0]
    return pl.pallas_call(
        fold_kernel,
        in_specs=[VMEM, VMEM],
        out_specs=VMEM,
        out_shape=jax.ShapeDtypeStruct((3, 4, 4 * depth, 4 * share), BF16),
        compiler_params=params(16),
        cost_estimate=cost(36 * depth * 256 * 128, 6 << 20),
        name="fold",
    )(w_root.transpose(2, 3, 4, 0, 1), w_root_in)


def y_window(j):
    return ((1, 0), (0, OCT), (1, OCT), (0, 2 * OCT))[j]


def place_kernel(offsets, padded, pairs, *refs):
    groups = len(offsets)
    pooled_refs, w_ref = refs[:groups], refs[groups]
    grid_ref, place_ref, pair_ref, step_ref = refs[groups + 1 : groups + 5]
    table = refs[groups + 5]
    depth = pooled_refs[0].shape[1]
    lane_count = groups * 128
    me = lax.axis_index("ga")
    row = lax.axis_index("row")

    metas = [r[SUBS * padded : SUBS * padded + META, :] for r in pooled_refs]
    parent = jnp.concatenate([m[0:1].astype(F32) for m in metas], axis=1).astype(jnp.int32)
    octant = jnp.concatenate([m[1:2].astype(F32) for m in metas], axis=1).astype(jnp.int32)
    found = jnp.zeros((META, lane_count), F32)
    for k, offset in enumerate(offsets):
        at = iota((128, lane_count), 0)
        hot = (at < pairs) & (parent == at + (me ^ offset) * pairs)
        found += dot(metas[k], jnp.where(hot, 1.0, 0.0).astype(BF16))
    block = found[2:3].astype(jnp.int32)
    side = RXY // HALF
    z = block // (side * side) * 2 + (octant >> 2)
    y = block // side % side * 2 + (octant >> 1) % 2
    x = block % side * 2 + octant % 2
    live = parent >= 0
    place = jnp.where(live, (z * OCT + y) * OCT + x, -1)
    place_ref[...] = jnp.broadcast_to(place, place_ref.shape)

    for k, pooled_ref in enumerate(pooled_refs):
        for v in range(SUBS):
            vz, vy, vx = v >> 2, v >> 1 & 1, v & 1
            lanes = slice((vx * 4 + vz * 2 + vy) * depth, (vx * 4 + vz * 2 + vy + 1) * depth)
            table[k * 128 : k * 128 + padded, lanes] = pooled_ref[v * padded : (v + 1) * padded, :]
            if padded < 128:
                table[k * 128 + padded : (k + 1) * 128, lanes] = jnp.zeros((128 - padded, depth), BF16)

    grid_ref[:, :, 0:OCT, :] = jnp.zeros((2, RZ_REG, OCT, 4 * depth), BF16)
    grid_ref[:, :, OCT + PLANE :, :] = jnp.zeros((2, RZ_REG, OCT, 4 * depth), BF16)
    shifted = (
        (0, 1, jnp.where(live & (x < OCT - 1), place + 1, -1)),
        (1, 0, place),
        (2, 1, place),
        (3, 0, jnp.where(live & (x > 0), place - 1, -1)),
    )
    for j, vx, at in shifted:
        hot = jnp.where(iota((LAYERS * PLANE, lane_count), 0) == at, 1.0, 0.0).astype(BF16)
        for vz in range(2):
            first = (vx * 4 + vz * 2) * depth
            both = dot(hot, table[:, first : first + 2 * depth]).astype(BF16)
            for vy in range(2):
                for layer in range(LAYERS):
                    grid_ref[vy, layer * 2 + vz, OCT : OCT + PLANE, j * depth : (j + 1) * depth] = both[
                        layer * PLANE : (layer + 1) * PLANE, vy * depth : (vy + 1) * depth
                    ]

    even = row % 2 == 0
    for out_ref, up in ((pair_ref, even), (step_ref, jnp.logical_not(even))):
        plane = jnp.where(up, RZ_REG - 1, 0)
        dz = jnp.where(up, 0, 2)
        total = None
        for j in range(4):
            vy, first = y_window(j)
            part = dot(grid_ref[vy, plane, first : first + PLANE, :], w_ref[dz, j])
            total = part if total is None else total + part
        out_ref[...] = total.astype(BF16)


def place(pooled, offsets, folded, padded, pairs):
    groups = len(offsets)
    depth = pooled[0].shape[1]
    wide = folded.shape[3]
    return pl.pallas_call(
        functools.partial(place_kernel, offsets, padded, pairs),
        in_specs=[VMEM] * (groups + 1),
        out_specs=[VMEM] * 4,
        out_shape=[
            jax.ShapeDtypeStruct((2, RZ_REG, BORDERED, 4 * depth), BF16),
            jax.ShapeDtypeStruct((8, groups * 128), jnp.int32),
            jax.ShapeDtypeStruct((PLANE, wide), BF16),
            jax.ShapeDtypeStruct((PLANE, wide), BF16),
        ],
        scratch_shapes=[pltpu.VMEM((groups * 128, SUBS * depth), BF16)],
        compiler_params=params(24),
        cost_estimate=cost(2 << 28, 6 << 20),
        name="place",
    )(*pooled, folded)


def conv_kernel(grid_ref, w_ref, out_ref):
    for z in range(RZ_REG):
        total = None
        for a in range(3):
            if not 0 <= z + a - 1 < RZ_REG:
                continue
            for j in range(4):
                vy, first = y_window(j)
                part = dot(grid_ref[vy, z + a - 1, first : first + PLANE, :], w_ref[a, j])
                total = part if total is None else total + part
        out_ref[z] = total


def conv(grid, folded):
    wide = folded.shape[3]
    return pl.pallas_call(
        conv_kernel,
        in_specs=[VMEM, VMEM],
        out_specs=VMEM,
        out_shape=jax.ShapeDtypeStruct((RZ_REG, PLANE, wide), F32),
        compiler_params=params(16),
        cost_estimate=cost(10 * 4 * PLANE * 512 * 256, 6 << 20),
        name="conv",
    )(grid, folded)


def finish_kernel(padded, place_ref, sums_ref, pair_ref, step_ref, bias_ref, *refs):
    groups = len(refs) - 2
    root_ref, empty_ref, send_refs = refs[0], refs[1], refs[2:]
    lane_count = place_ref.shape[1]
    row = lax.axis_index("row")
    even = row % 2 == 0
    last = lax.axis_size("row") - 1
    bias = jnp.concatenate([bias_ref[...]] * 4, axis=1)
    pair = pair_ref[...].astype(F32)
    step = step_ref[...].astype(F32)
    above = jnp.where(even, pair, step)
    below = jnp.where(even, step, pair)
    above = jnp.where(row < last, above, 0.0)
    below = jnp.where(row > 0, below, 0.0)
    column = place_ref[...].astype(F32).T[:, 0:1].astype(jnp.int32)
    empty_ref[...] = jnp.broadcast_to(jnp.where(column[0:padded] < 0, -1e30, 0.0), empty_ref.shape)
    hot = jnp.where(column == iota((lane_count, LAYERS * PLANE), 1), 1.0, 0.0).astype(BF16)
    for z in range(RZ_REG):
        total = sums_ref[z] + bias
        if z == 0:
            total += below
        if z == RZ_REG - 1:
            total += above
        root_ref[z % 2, z // 2 * PLANE : (z // 2 + 1) * PLANE, :] = jnp.maximum(total, 0.0).astype(BF16)
    wide = root_ref.shape[2]
    for vz in range(2):
        picked = dot(hot, root_ref[vz]).astype(BF16)
        for k in range(groups):
            send_refs[k][:, vz * wide : (vz + 1) * wide] = picked[k * 128 : k * 128 + padded]


def finish(places, sums, pair, step, root_bias, groups, padded):
    wide = sums.shape[2]
    return pl.pallas_call(
        functools.partial(finish_kernel, padded),
        in_specs=[VMEM] * 5,
        out_specs=[VMEM] * (groups + 2),
        out_shape=[
            jax.ShapeDtypeStruct((2, LAYERS * PLANE, wide), BF16),
            jax.ShapeDtypeStruct((padded, 128), F32),
        ]
        + [jax.ShapeDtypeStruct((padded, 2 * wide), BF16)] * groups,
        compiler_params=params(24),
        cost_estimate=cost(1 << 27, 3 << 20),
        name="finish",
    )(places, sums, pair, step, root_bias[None])


def unravel_kernel(offsets, root_ref, down_ref, skip_ref, out_ref, lift_ref, weights_ref, spread_ref):
    share = root_ref.shape[2] // 4
    rows, half = PLANE, PLANE // 2
    x, y = iota((rows, half), 0), iota((rows, half), 1)
    same = x // RXY == y // OCT
    spread = [
        jnp.where(same & (x % RXY == 2 * (y % OCT) + vx), 1.0, 0.0).astype(BF16) for vx in range(2)
    ]
    lines = half // OCT
    for z in range(RZ_REG):
        for part in range(2):
            first = z // 2 * PLANE + part * half
            for vy in range(2):
                at = vy * 2 * share
                even = root_ref[z % 2, first : first + half, at : at + share]
                odd = root_ref[z % 2, first : first + half, at + share : at + 2 * share]
                line = (dot(spread[0], even) + dot(spread[1], odd)).astype(BF16)
                out_ref[z, part * lines : (part + 1) * lines, vy] = line.reshape(lines, RXY, share)

    me = lax.axis_index("ga")
    width, depth = skip_ref.shape
    lift_ref[...] = jnp.zeros_like(lift_ref)
    for k, offset in enumerate(offsets):
        own = down_ref[pl.ds(pl.multiple_of((me ^ offset) * share, share), share), :]
        for vx in range(2):
            first = (k * 2 + vx) * share
            lift_ref[first : first + share, vx * depth : (vx + 1) * depth] = own
    weights_ref[...] = jnp.zeros_like(weights_ref)
    turned = skip_ref[...].T
    for s in range(weights_ref.shape[0] // depth):
        weights_ref[s * depth : (s + 1) * depth, s * width : (s + 1) * width] = turned
    hit = hidden_voxel(iota(spread_ref.shape, 1)) == iota(spread_ref.shape, 0)
    spread_ref[...] = jnp.where(hit, 1.0, 0.0).astype(BF16)


def unravel(root, w_down, w_skip, offsets, voxels):
    share = root.shape[2] // 4
    depth, width = w_skip.shape
    group = 256 // width
    out, lift, weights, spread = pl.pallas_call(
        functools.partial(unravel_kernel, offsets),
        in_specs=[VMEM] * 3,
        out_specs=[VMEM] * 4,
        out_shape=[
            jax.ShapeDtypeStruct((RZ_REG, OCT, 2, RXY, share), BF16),
            jax.ShapeDtypeStruct((len(offsets) * 2 * share, 2 * depth), BF16),
            jax.ShapeDtypeStruct((group * depth, group * width), BF16),
            jax.ShapeDtypeStruct((voxels // SUBS, voxels), BF16),
        ],
        compiler_params=params(12),
        cost_estimate=cost(1 << 28, 2 << 20),
        name="unravel",
    )(root, w_down, w_skip.T)
    return out.reshape(RZ_REG, RXY, RXY, share).transpose(3, 0, 1, 2), lift, weights, spread


def fine_out_kernel(groups, *refs):
    fine_ref, hidden_ref, empty_ref, lift_ref, weights_ref, spread_ref = refs[:6]
    come_refs = refs[6 : 6 + groups]
    out_hbm, out_ref, lifted, skips, sems = refs[6 + groups :]
    total, width, voxels = fine_ref.shape
    depth = lift_ref.shape[1] // 2
    group = hidden_ref.shape[2] // depth
    cells = voxels // SUBS
    share = come_refs[0].shape[1] // SUBS
    chunk = total // sems.shape[0]
    sets = chunk // group

    for zy in range(4):
        lanes = slice(zy * 2 * share, (zy + 1) * 2 * share)
        both = dot(jnp.concatenate([r[:, lanes] for r in come_refs], axis=1), lift_ref[...])
        slots = both.shape[0]
        for vx in range(2):
            top = both[:, vx * depth : (vx + 1) * depth] + empty_ref[...]
            lifted[pl.ds(zy * 2 + vx, slots, stride=SUBS), :] = top

    for i in range(total // chunk):
        rows = []
        for g in range(sets):
            at = i * sets + g
            tops = [
                lifted[(at * group + s) * SUBS : (at * group + s + 1) * SUBS, :] for s in range(group)
            ]
            hidden = hidden_ref[at].astype(F32).reshape(SUBS, SUBS, group * depth)
            decoded = jnp.maximum(hidden + jnp.concatenate(tops, axis=1)[None], 0.0)
            rows.append(decoded.reshape(cells, group * depth).astype(BF16))
        skip = dot(jnp.concatenate(rows, axis=0), weights_ref[...]).astype(BF16)
        for g in range(sets):
            at = (i * sets + g) * group * width
            skips[at : at + group * width, :] = skip[g * cells : (g + 1) * cells].T

    def send(i):
        part = pl.ds(i * chunk, chunk)
        return pltpu.make_async_copy(out_ref.at[part], out_hbm.at[part], sems.at[i])

    for i in range(total // chunk):
        part = slice(i * chunk, (i + 1) * chunk)
        up = dot(skips[i * chunk * width : (i + 1) * chunk * width, :], spread_ref[...])
        cube = fine_ref[part].reshape(chunk * width, voxels)
        out_ref[part] = (cube.astype(F32) + up).astype(BF16).reshape(chunk, width, voxels)
        send(i).start()
    for i in range(total // chunk):
        send(i).wait()


def fine_out(fine_feats, hidden, empty, lift, weights, spread, come):
    total, width, voxels = fine_feats.shape
    padded = empty.shape[0]
    depth = lift.shape[1] // 2
    group = 256 // width
    groups = len(come)
    chunk = parts_of(total, group, 16)
    return pl.pallas_call(
        functools.partial(fine_out_kernel, groups),
        in_specs=[VMEM] * (6 + groups),
        out_specs=ANY,
        out_shape=jax.ShapeDtypeStruct(fine_feats.shape, BF16),
        scratch_shapes=[
            pltpu.VMEM(fine_feats.shape, BF16),
            pltpu.VMEM((padded * SUBS, depth), F32),
            pltpu.VMEM((total * width, voxels // SUBS), BF16),
            pltpu.SemaphoreType.DMA((total // chunk,)),
        ],
        compiler_params=params(28),
        cost_estimate=cost(total * width * voxels * 256, 4 * total * width * voxels),
        name="fine_out",
    )(fine_feats, hidden, empty, lift, weights, spread, *come)


def shards(
    fine_feats, fine_child, parent_block, w_parent, w_root_in, w_root, root_bias, w_down, w_skip
):
    groups = lax.axis_size("ga")
    rows = lax.axis_size("row")
    slots = fine_feats.shape[0]
    padded = -(-slots // META) * META
    pairs = parent_block.shape[0]

    hidden, pooled = fine_in(fine_feats, fine_child, parent_block, w_parent, padded)

    gathered, offsets = [pooled], [0]
    bit = groups // 2
    while bit:
        swap = [(i, i ^ bit) for i in range(groups)]
        gathered += [lax.ppermute(part, "ga", swap) for part in gathered]
        offsets += [offset ^ bit for offset in offsets]
        bit //= 2
    offsets = tuple(offsets)

    folded = fold(w_root, w_root_in)
    grid, places, pair, step = place(gathered, offsets, folded, padded, pairs)
    pair_swap = [(i, i ^ 1) for i in range(rows) if i ^ 1 < rows]
    step_swap = [(i, (i - 1 ^ 1) + 1) for i in range(1, rows) if (i - 1 ^ 1) + 1 < rows]
    pair = lax.ppermute(pair, "row", pair_swap)
    step = lax.ppermute(step, "row", step_swap)
    sums = conv(grid, folded)
    root, empty, *sends = finish(places, sums, pair, step, root_bias, groups, padded)
    come = [sends[0]]
    for offset, send in zip(offsets[1:], sends[1:]):
        come.append(lax.ppermute(send, "ga", [(i, i ^ offset) for i in range(groups)]))
    root_out, lift, weights, spread = unravel(root, w_down, w_skip, offsets, fine_feats.shape[2])
    fine = fine_out(fine_feats, hidden, empty, lift, weights, spread, come)
    return (fine, root_out)


def solution(mesh):
    return jax.shard_map(
        shards,
        mesh=mesh,
        in_specs=(
            P(("row", "ga"), None, None),
            P(("row", "ga")),
            P(("row", "ga")),
            P(),
            P(),
            P("ga", None, None, None, None),
            P("ga"),
            P(),
            P(),
        ),
        out_specs=(P(("row", "ga"), None, None), P("ga", "row", None, None)),
        check_vma=False,
    )
```

```python
import functools

import jax
import jax.numpy as jnp
from jax import lax
from jax.experimental import pallas as pl
from jax.experimental.pallas import tpu as pltpu
from jax.sharding import PartitionSpec as P

B = 8
RXY = 32
RZ_REG = 4

HALF = B // 2
OCT = RXY // 2
LAYERS = RZ_REG // 2
PLANE = OCT * OCT
BORDERED = PLANE + 2 * OCT
SUBS = 8
META = 16
BF16 = jnp.bfloat16
F32 = jnp.float32
VMEM = pl.BlockSpec(memory_space=pltpu.VMEM)
ANY = pl.BlockSpec(memory_space=pl.ANY)


def params(mib):
    return pltpu.CompilerParams(vmem_limit_bytes=mib << 20)


def cost(macs, moved):
    return pl.CostEstimate(flops=2 * macs, bytes_accessed=moved, transcendentals=0)


def iota(shape, axis):
    return lax.broadcasted_iota(jnp.int32, shape, axis)


def dot(left, right):
    return jnp.dot(left, right, preferred_element_type=F32)


def dot_nt(left, right):
    return lax.dot_general(left, right, (((1,), (1,)), ((), ())), preferred_element_type=F32)


def hidden_voxel(fine):
    edge = B.bit_length() - 1
    z, y, x = fine >> 2 * edge, fine >> edge & B - 1, fine & B - 1
    low = (z >> 1 & 1) * 4 + (y >> 1 & 1) * 2 + (x >> 1 & 1)
    high = (z >> edge - 1) * 4 + (y >> edge - 1) * 2 + (x >> edge - 1)
    return low * SUBS + high


def run_bounds(count):
    cuts = [0]
    while cuts[-1] < count:
        cuts.append(min(2 * cuts[-1] + 1, count))
    return list(zip(cuts, cuts[1:]))


def repeat_blocks(ref, block):
    rows, columns = block.shape
    ref[...] = jnp.zeros_like(ref)
    for s in range(ref.shape[0] // rows):
        ref[s * rows : (s + 1) * rows, s * columns : (s + 1) * columns] = block


def parts_of(total, group, most):
    return max(n for n in range(group, most + 1, group) if total % n == 0)


def fine_in_kernel(
    child_hbm, block_hbm, fine_hbm, w_hbm, turned_hbm, pooled_ref,
    fine_ref, child_ref, block_ref, w_ref, pool, weights, turned, tops, meta, fine_sems, turned_sems, sems, *, total, padded
):
    _, width, voxels = fine_ref.shape
    depth = w_ref.shape[1]
    group = turned.shape[1] // width
    cells = voxels // SUBS
    chunk = total // fine_sems.shape[0]
    sets = chunk // group

    def fetch(i):
        part = pl.ds(i * chunk, chunk)
        return pltpu.make_async_copy(fine_hbm.at[part], fine_ref.at[part], fine_sems.at[i])

    def store(low, high):
        part = pl.ds(low * sets * cells, (high - low) * sets * cells)
        return pltpu.make_async_copy(turned.at[part], turned_hbm.at[part], turned_sems.at[low])

    fetch(0).start(priority=1)
    small = [
        pltpu.make_async_copy(source, target, sems.at[i])
        for i, (source, target) in enumerate(
            ((w_hbm, w_ref), (child_hbm, child_ref), (block_hbm, block_ref))
        )
    ]
    for copy in small:
        copy.start()
    for i in range(1, total // chunk):
        fetch(i).start(priority=1)

    hit = hidden_voxel(iota((voxels, cells), 0)) == iota((voxels, cells), 1)
    pool[...] = jnp.where(hit, 1.0 / SUBS, 0.0).astype(BF16)
    for copy in small:
        copy.wait()
    repeat_blocks(weights, w_ref[...])
    meta[...] = jnp.full_like(meta, -1.0)
    meta[0:1, 0:total] = (child_ref[...] >> 3).astype(F32)
    meta[1:2, 0:total] = (child_ref[...] & 7).astype(F32)
    meta[2:3, 0 : block_ref.shape[1]] = block_ref[...].astype(F32)
    pooled_ref[SUBS * padded : SUBS * padded + META, :] = meta[...].astype(BF16)

    runs = run_bounds(total // chunk)
    for low, high in runs:
        for i in range(low, high):
            fetch(i).wait()
        cube = fine_ref[low * chunk : high * chunk].reshape((high - low) * chunk * width, voxels)
        octants = dot(cube, pool[...]).astype(BF16)
        for g in range((high - low) * sets):
            at = (low * sets + g) * cells
            turned[at : at + cells, :] = octants[g * group * width : (g + 1) * group * width].T
        store(low, high).start()
    for low, high in runs:
        rows = turned[low * sets * cells : high * sets * cells, :]
        hidden = jnp.maximum(dot(rows, weights[...]), 0.0).astype(BF16)
        cubes = hidden.astype(F32).reshape((high - low) * sets, SUBS, SUBS, group * depth)
        top = jnp.sum(cubes, axis=1) * (1.0 / SUBS)
        for g in range((high - low) * sets):
            for s in range(group):
                at = (low * chunk + g * group + s) * SUBS
                tops[at : at + SUBS, :] = top[g, :, s * depth : (s + 1) * depth]
    if padded != total:
        tops[total * SUBS :, :] = jnp.zeros(((padded - total) * SUBS, depth), F32)
    for v in range(SUBS):
        pooled_ref[v * padded : (v + 1) * padded, :] = tops[pl.ds(v, padded, stride=SUBS), :].astype(BF16)
    for low, high in runs:
        store(low, high).wait()


def fine_in(fine_feats, fine_child, parent_block, w_parent, padded):
    total, width, voxels = fine_feats.shape
    depth = w_parent.shape[1]
    pairs = parent_block.shape[0]
    group = 256 // width
    cells = voxels // SUBS
    chunk = parts_of(total, group, 16)
    return pl.pallas_call(
        functools.partial(fine_in_kernel, total=total, padded=padded),
        in_specs=[ANY] * 4,
        out_specs=[ANY, VMEM],
        out_shape=[
            jax.ShapeDtypeStruct((total // group * cells, group * width), BF16),
            jax.ShapeDtypeStruct((SUBS * padded + META, depth), BF16),
        ],
        scratch_shapes=[
            pltpu.VMEM(fine_feats.shape, BF16),
            pltpu.VMEM((1, total), jnp.int32),
            pltpu.VMEM((1, pairs), jnp.int32),
            pltpu.VMEM(w_parent.shape, BF16),
            pltpu.VMEM((voxels, cells), BF16),
            pltpu.VMEM((group * width, group * depth), BF16),
            pltpu.VMEM((total // group * cells, group * width), BF16),
            pltpu.VMEM((padded * SUBS, depth), F32),
            pltpu.VMEM((META, 128), F32),
            pltpu.SemaphoreType.DMA((total // chunk,)),
            pltpu.SemaphoreType.DMA((total // chunk,)),
            pltpu.SemaphoreType.DMA((3,)),
        ],
        compiler_params=params(58),
        cost_estimate=cost(total * width * voxels * 256, 2 * total * width * voxels),
        name="fine_in",
    )(fine_child[None], parent_block[None], fine_feats, w_parent)


def hide_kernel(turned_ref, w_ref, hidden_ref, weights):
    repeat_blocks(weights, w_ref[...])
    hidden_ref[...] = jnp.maximum(dot(turned_ref[...], weights[...]), 0.0).astype(BF16)


def hide(turned, w_parent):
    width, depth = w_parent.shape
    rows, wide = turned.shape
    return pl.pallas_call(
        hide_kernel,
        in_specs=[VMEM] * 2,
        out_specs=VMEM,
        out_shape=jax.ShapeDtypeStruct((rows, wide // width * depth), BF16),
        scratch_shapes=[pltpu.VMEM((wide, wide // width * depth), BF16)],
        compiler_params=params(12),
        cost_estimate=cost(rows * wide * 512, rows * wide * 6),
        name="hide",
    )(turned, w_parent)


def fold_kernel(w_ref, in_ref, out_ref):
    share = w_ref.shape[3]
    depth = in_ref.shape[0]
    nothing = jnp.zeros((share, w_ref.shape[4]), BF16)
    out_ref[:, 0, :, 2 * share :] = jnp.zeros((3, 4 * depth, 2 * share), BF16)
    out_ref[:, 3, :, 0 : 2 * share] = jnp.zeros((3, 4 * depth, 2 * share), BF16)
    for a in range(3):
        for b in range(3):
            for j in range(4):
                first = w_ref[a, b, j] if j < 3 else nothing
                second = w_ref[a, b, j - 1] if j > 0 else nothing
                pair = jnp.concatenate([first, second], axis=0)
                folded = dot_nt(in_ref[...], pair).astype(BF16)
                rows = slice(j * depth, (j + 1) * depth)
                out_ref[a, b, rows, 0 : 2 * share] = folded
                out_ref[a, b + 1, rows, 2 * share : 4 * share] = folded


def fold(w_root, w_root_in):
    share = w_root.shape[0]
    depth = w_root_in.shape[0]
    return pl.pallas_call(
        fold_kernel,
        in_specs=[VMEM, VMEM],
        out_specs=VMEM,
        out_shape=jax.ShapeDtypeStruct((3, 4, 4 * depth, 4 * share), BF16),
        compiler_params=params(16),
        cost_estimate=cost(36 * depth * 256 * 128, 6 << 20),
        name="fold",
    )(w_root.transpose(2, 3, 4, 0, 1), w_root_in)


def y_window(j):
    return ((1, 0), (0, OCT), (1, OCT), (0, 2 * OCT))[j]


def place_kernel(offsets, padded, pairs, *refs):
    groups = len(offsets)
    pooled_refs, w_ref = refs[:groups], refs[groups]
    grid_ref, place_ref, pair_ref, step_ref = refs[groups + 1 : groups + 5]
    table = refs[groups + 5]
    depth = pooled_refs[0].shape[1]
    lane_count = groups * 128
    me = lax.axis_index("ga")
    row = lax.axis_index("row")

    metas = [r[SUBS * padded : SUBS * padded + META, :] for r in pooled_refs]
    parent = jnp.concatenate([m[0:1].astype(F32) for m in metas], axis=1).astype(jnp.int32)
    octant = jnp.concatenate([m[1:2].astype(F32) for m in metas], axis=1).astype(jnp.int32)
    found = jnp.zeros((META, lane_count), F32)
    for k, offset in enumerate(offsets):
        at = iota((128, lane_count), 0)
        hot = (at < pairs) & (parent == at + (me ^ offset) * pairs)
        found += dot(metas[k], jnp.where(hot, 1.0, 0.0).astype(BF16))
    block = found[2:3].astype(jnp.int32)
    side = RXY // HALF
    z = block // (side * side) * 2 + (octant >> 2)
    y = block // side % side * 2 + (octant >> 1) % 2
    x = block % side * 2 + octant % 2
    live = parent >= 0
    place = jnp.where(live, (z * OCT + y) * OCT + x, -1)
    place_ref[...] = jnp.broadcast_to(place, place_ref.shape)

    for k, pooled_ref in enumerate(pooled_refs):
        for v in range(SUBS):
            vz, vy, vx = v >> 2, v >> 1 & 1, v & 1
            lanes = slice((vx * 4 + vz * 2 + vy) * depth, (vx * 4 + vz * 2 + vy + 1) * depth)
            table[k * 128 : k * 128 + padded, lanes] = pooled_ref[v * padded : (v + 1) * padded, :]
            if padded < 128:
                table[k * 128 + padded : (k + 1) * 128, lanes] = jnp.zeros((128 - padded, depth), BF16)

    grid_ref[:, :, 0:OCT, :] = jnp.zeros((2, RZ_REG, OCT, 4 * depth), BF16)
    grid_ref[:, :, OCT + PLANE :, :] = jnp.zeros((2, RZ_REG, OCT, 4 * depth), BF16)
    shifted = (
        (0, 1, jnp.where(live & (x < OCT - 1), place + 1, -1)),
        (1, 0, place),
        (2, 1, place),
        (3, 0, jnp.where(live & (x > 0), place - 1, -1)),
    )
    for j, vx, at in shifted:
        hot = jnp.where(iota((LAYERS * PLANE, lane_count), 0) == at, 1.0, 0.0).astype(BF16)
        for vz in range(2):
            first = (vx * 4 + vz * 2) * depth
            both = dot(hot, table[:, first : first + 2 * depth]).astype(BF16)
            for vy in range(2):
                for layer in range(LAYERS):
                    grid_ref[vy, layer * 2 + vz, OCT : OCT + PLANE, j * depth : (j + 1) * depth] = both[
                        layer * PLANE : (layer + 1) * PLANE, vy * depth : (vy + 1) * depth
                    ]

    even = row % 2 == 0
    for out_ref, up in ((pair_ref, even), (step_ref, jnp.logical_not(even))):
        plane = jnp.where(up, RZ_REG - 1, 0)
        dz = jnp.where(up, 0, 2)
        total = None
        for j in range(4):
            vy, first = y_window(j)
            part = dot(grid_ref[vy, plane, first : first + PLANE, :], w_ref[dz, j])
            total = part if total is None else total + part
        out_ref[...] = total.astype(BF16)


def place(pooled, offsets, folded, padded, pairs):
    groups = len(offsets)
    depth = pooled[0].shape[1]
    wide = folded.shape[3]
    return pl.pallas_call(
        functools.partial(place_kernel, offsets, padded, pairs),
        in_specs=[VMEM] * (groups + 1),
        out_specs=[VMEM] * 4,
        out_shape=[
            jax.ShapeDtypeStruct((2, RZ_REG, BORDERED, 4 * depth), BF16),
            jax.ShapeDtypeStruct((8, groups * 128), jnp.int32),
            jax.ShapeDtypeStruct((PLANE, wide), BF16),
            jax.ShapeDtypeStruct((PLANE, wide), BF16),
        ],
        scratch_shapes=[pltpu.VMEM((groups * 128, SUBS * depth), BF16)],
        compiler_params=params(24),
        cost_estimate=cost(2 << 28, 6 << 20),
        name="place",
    )(*pooled, folded)


def conv_kernel(grid_ref, w_ref, out_ref):
    for z in range(RZ_REG):
        total = None
        for a in range(3):
            if not 0 <= z + a - 1 < RZ_REG:
                continue
            for j in range(4):
                vy, first = y_window(j)
                part = dot(grid_ref[vy, z + a - 1, first : first + PLANE, :], w_ref[a, j])
                total = part if total is None else total + part
        out_ref[z] = total


def conv(grid, folded):
    wide = folded.shape[3]
    return pl.pallas_call(
        conv_kernel,
        in_specs=[VMEM, VMEM],
        out_specs=VMEM,
        out_shape=jax.ShapeDtypeStruct((RZ_REG, PLANE, wide), F32),
        compiler_params=params(16),
        cost_estimate=cost(10 * 4 * PLANE * 512 * 256, 6 << 20),
        name="conv",
    )(grid, folded)


def finish_kernel(padded, order, place_ref, sums_ref, pair_ref, step_ref, bias_ref, *refs):
    root_ref, empty_ref, send_refs = refs[0], refs[1], refs[2:]
    lane_count = place_ref.shape[1]
    row = lax.axis_index("row")
    even = row % 2 == 0
    last = lax.axis_size("row") - 1
    bias = jnp.concatenate([bias_ref[...]] * 4, axis=1)
    pair = pair_ref[...].astype(F32)
    step = step_ref[...].astype(F32)
    above = jnp.where(even, pair, step)
    below = jnp.where(even, step, pair)
    above = jnp.where(row < last, above, 0.0)
    below = jnp.where(row > 0, below, 0.0)
    column = place_ref[...].astype(F32).T[:, 0:1].astype(jnp.int32)
    empty_ref[...] = jnp.broadcast_to(jnp.where(column[0:padded] < 0, -1e30, 0.0), empty_ref.shape)
    hot = jnp.where(column == iota((lane_count, LAYERS * PLANE), 1), 1.0, 0.0).astype(BF16)
    for z in range(RZ_REG):
        total = sums_ref[z] + bias
        if z == 0:
            total += below
        if z == RZ_REG - 1:
            total += above
        root_ref[z % 2, z // 2 * PLANE : (z // 2 + 1) * PLANE, :] = jnp.maximum(total, 0.0).astype(BF16)
    wide = root_ref.shape[2]
    for vz in range(2):
        picked = dot(hot, root_ref[vz]).astype(BF16)
        for send_ref, k in zip(send_refs, order):
            send_ref[:, vz * wide : (vz + 1) * wide] = picked[k * 128 : k * 128 + padded]


def finish(places, sums, pair, step, root_bias, order, padded):
    wide = sums.shape[2]
    groups = len(order)
    return pl.pallas_call(
        functools.partial(finish_kernel, padded, order),
        in_specs=[VMEM] * 5,
        out_specs=[VMEM] * (groups + 2),
        out_shape=[
            jax.ShapeDtypeStruct((2, LAYERS * PLANE, wide), BF16),
            jax.ShapeDtypeStruct((padded, 128), F32),
        ]
        + [jax.ShapeDtypeStruct((padded, 2 * wide), BF16)] * groups,
        compiler_params=params(24),
        cost_estimate=cost(1 << 27, 3 << 20),
        name="finish",
    )(places, sums, pair, step, root_bias[None])


def unravel_kernel(offsets, root_ref, down_ref, skip_ref, out_ref, lift_ref, weights_ref, spread_ref):
    share = root_ref.shape[2] // 4
    rows, half = PLANE, PLANE // 2
    x, y = iota((rows, half), 0), iota((rows, half), 1)
    same = x // RXY == y // OCT
    spread = [
        jnp.where(same & (x % RXY == 2 * (y % OCT) + vx), 1.0, 0.0).astype(BF16) for vx in range(2)
    ]
    lines = half // OCT
    for z in range(RZ_REG):
        for part in range(2):
            first = z // 2 * PLANE + part * half
            for vy in range(2):
                at = vy * 2 * share
                even = root_ref[z % 2, first : first + half, at : at + share]
                odd = root_ref[z % 2, first : first + half, at + share : at + 2 * share]
                line = (dot(spread[0], even) + dot(spread[1], odd)).astype(BF16)
                out_ref[z, part * lines : (part + 1) * lines, vy] = line.reshape(lines, RXY, share)

    me = lax.axis_index("ga")
    width, depth = skip_ref.shape
    lift_ref[...] = jnp.zeros_like(lift_ref)
    for k, offset in enumerate(offsets):
        own = down_ref[pl.ds(pl.multiple_of((me ^ offset) * share, share), share), :]
        for vx in range(2):
            first = (k * 2 + vx) * share
            lift_ref[first : first + share, vx * depth : (vx + 1) * depth] = own
    repeat_blocks(weights_ref, skip_ref[...].T)
    hit = hidden_voxel(iota(spread_ref.shape, 1)) == iota(spread_ref.shape, 0)
    spread_ref[...] = jnp.where(hit, 1.0, 0.0).astype(BF16)


def unravel(root, w_down, w_skip, offsets, voxels):
    share = root.shape[2] // 4
    depth, width = w_skip.shape
    group = 256 // width
    out, lift, weights, spread = pl.pallas_call(
        functools.partial(unravel_kernel, offsets),
        in_specs=[VMEM] * 3,
        out_specs=[VMEM] * 4,
        out_shape=[
            jax.ShapeDtypeStruct((RZ_REG, OCT, 2, RXY, share), BF16),
            jax.ShapeDtypeStruct((len(offsets) * 2 * share, 2 * depth), BF16),
            jax.ShapeDtypeStruct((group * depth, group * width), BF16),
            jax.ShapeDtypeStruct((voxels // SUBS, voxels), BF16),
        ],
        compiler_params=params(12),
        cost_estimate=cost(1 << 28, 2 << 20),
        name="unravel",
    )(root, w_down, w_skip.T)
    return out.reshape(RZ_REG, RXY, RXY, share).transpose(3, 0, 1, 2), lift, weights, spread


def fine_out_kernel(groups, *refs):
    fine_ref, hidden_ref, empty_ref, lift_ref, weights_ref, spread_ref = refs[:6]
    come_refs = refs[6 : 6 + groups]
    out_hbm, out_ref, lifted, skips, sems = refs[6 + groups :]
    total, width, voxels = fine_ref.shape
    depth = lift_ref.shape[1] // 2
    group = hidden_ref.shape[1] // depth
    cells = voxels // SUBS
    share = come_refs[0].shape[1] // SUBS
    chunk = total // sems.shape[0]
    sets = chunk // group

    for zy in range(4):
        lanes = slice(zy * 2 * share, (zy + 1) * 2 * share)
        both = dot(jnp.concatenate([r[:, lanes] for r in come_refs], axis=1), lift_ref[...])
        slots = both.shape[0]
        for vx in range(2):
            top = both[:, vx * depth : (vx + 1) * depth] + empty_ref[...]
            lifted[pl.ds(zy * 2 + vx, slots, stride=SUBS), :] = top

    for i in range(total // chunk):
        rows = []
        for g in range(sets):
            at = i * sets + g
            tops = [
                lifted[(at * group + s) * SUBS : (at * group + s + 1) * SUBS, :] for s in range(group)
            ]
            hidden = hidden_ref[at * cells : (at + 1) * cells, :].astype(F32).reshape(SUBS, SUBS, group * depth)
            decoded = jnp.maximum(hidden + jnp.concatenate(tops, axis=1)[None], 0.0)
            rows.append(decoded.reshape(cells, group * depth).astype(BF16))
        skip = dot(jnp.concatenate(rows, axis=0), weights_ref[...]).astype(BF16)
        for g in range(sets):
            at = (i * sets + g) * group * width
            skips[at : at + group * width, :] = skip[g * cells : (g + 1) * cells].T

    def send(i):
        part = pl.ds(i * chunk, chunk)
        return pltpu.make_async_copy(out_ref.at[part], out_hbm.at[part], sems.at[i])

    for i in range(total // chunk):
        part = slice(i * chunk, (i + 1) * chunk)
        up = dot(skips[i * chunk * width : (i + 1) * chunk * width, :], spread_ref[...])
        cube = fine_ref[part].reshape(chunk * width, voxels)
        out_ref[part] = (cube.astype(F32) + up).astype(BF16).reshape(chunk, width, voxels)
        send(i).start()
    for i in range(total // chunk):
        send(i).wait()


def fine_out(fine_feats, hidden, empty, lift, weights, spread, come):
    total, width, voxels = fine_feats.shape
    padded = empty.shape[0]
    depth = lift.shape[1] // 2
    group = 256 // width
    groups = len(come)
    chunk = parts_of(total, group, 16)
    return pl.pallas_call(
        functools.partial(fine_out_kernel, groups),
        in_specs=[VMEM] * (6 + groups),
        out_specs=ANY,
        out_shape=jax.ShapeDtypeStruct(fine_feats.shape, BF16),
        scratch_shapes=[
            pltpu.VMEM(fine_feats.shape, BF16),
            pltpu.VMEM((padded * SUBS, depth), F32),
            pltpu.VMEM((total * width, voxels // SUBS), BF16),
            pltpu.SemaphoreType.DMA((total // chunk,)),
        ],
        compiler_params=params(28),
        cost_estimate=cost(total * width * voxels * 256, 4 * total * width * voxels),
        name="fine_out",
    )(fine_feats, hidden, empty, lift, weights, spread, *come)


def shards(
    fine_feats, fine_child, parent_block, w_parent, w_root_in, w_root, root_bias, w_down, w_skip
):
    groups = lax.axis_size("ga")
    rows = lax.axis_size("row")
    slots = fine_feats.shape[0]
    padded = -(-slots // META) * META
    pairs = parent_block.shape[0]

    turned, pooled = fine_in(fine_feats, fine_child, parent_block, w_parent, padded)

    hidden = hide(turned, w_parent)
    folded = fold(w_root, w_root_in)

    gathered, offsets = [pooled], [0]
    bit = groups // 2
    while bit:
        swap = [(i, i ^ bit) for i in range(groups)]
        gathered += [lax.ppermute(part, "ga", swap) for part in gathered]
        offsets += [offset ^ bit for offset in offsets]
        if bit == groups // 2:
            gathered[1], folded, hidden = lax.optimization_barrier((gathered[1], folded, hidden))
        bit //= 2
    offsets = tuple(offsets)

    grid, places, pair, step = place(gathered, offsets, folded, padded, pairs)
    pair_swap = [(i, i ^ 1) for i in range(rows) if i ^ 1 < rows]
    step_swap = [(i, (i - 1 ^ 1) + 1) for i in range(1, rows) if (i - 1 ^ 1) + 1 < rows]
    pair = lax.ppermute(pair, "row", pair_swap)
    step = lax.ppermute(step, "row", step_swap)
    sums = conv(grid, folded)
    order = sorted(range(groups), key=lambda k: (offsets[k] > 0, offsets[k] < groups // 2, offsets[k]))
    root, empty, *sends = finish(places, sums, pair, step, root_bias, order, padded)
    come = sends[:1]
    for k, send in zip(order[1:], sends[1:]):
        come.append(lax.ppermute(send, "ga", [(i, i ^ offsets[k]) for i in range(groups)]))
    root_out, lift, weights, spread = unravel(
        root, w_down, w_skip, [offsets[k] for k in order], fine_feats.shape[2]
    )
    fine = fine_out(fine_feats, hidden, empty, lift, weights, spread, come)
    return (fine, root_out)


def solution(mesh):
    return jax.shard_map(
        shards,
        mesh=mesh,
        in_specs=(
            P(("row", "ga"), None, None),
            P(("row", "ga")),
            P(("row", "ga")),
            P(),
            P(),
            P("ga", None, None, None, None),
            P("ga"),
            P(),
            P(),
        ),
        out_specs=(P(("row", "ga"), None, None), P("ga", "row", None, None)),
        check_vma=False,
    )
```

```python
import functools

import jax
import jax.numpy as jnp
from jax import lax
from jax.experimental import pallas as pl
from jax.experimental.pallas import tpu as pltpu
from jax.sharding import PartitionSpec as P

B = 8
RXY = 32
RZ_REG = 4

HALF = B // 2
OCT = RXY // 2
LAYERS = RZ_REG // 2
PLANE = OCT * OCT
BORDERED = PLANE + 2 * OCT
SUBS = 8
META = 16
BF16 = jnp.bfloat16
F32 = jnp.float32
VMEM = pl.BlockSpec(memory_space=pltpu.VMEM)
ANY = pl.BlockSpec(memory_space=pl.ANY)


def params(mib):
    return pltpu.CompilerParams(vmem_limit_bytes=mib << 20)


def cost(macs, moved):
    return pl.CostEstimate(flops=2 * macs, bytes_accessed=moved, transcendentals=0)


def iota(shape, axis):
    return lax.broadcasted_iota(jnp.int32, shape, axis)


def dot(left, right):
    return jnp.dot(left, right, preferred_element_type=F32)


def dot_nt(left, right):
    return lax.dot_general(left, right, (((1,), (1,)), ((), ())), preferred_element_type=F32)


def hidden_voxel(fine):
    edge = B.bit_length() - 1
    z, y, x = fine >> 2 * edge, fine >> edge & B - 1, fine & B - 1
    low = (z >> 1 & 1) * 4 + (y >> 1 & 1) * 2 + (x >> 1 & 1)
    high = (z >> edge - 1) * 4 + (y >> edge - 1) * 2 + (x >> edge - 1)
    return low * SUBS + high


def run_bounds(count):
    cuts = [0]
    while cuts[-1] < count:
        cuts.append(min(2 * cuts[-1] + 1, count))
    return list(zip(cuts, cuts[1:]))


def repeat_blocks(ref, block):
    rows, columns = block.shape
    ref[...] = jnp.zeros_like(ref)
    for s in range(ref.shape[0] // rows):
        ref[s * rows : (s + 1) * rows, s * columns : (s + 1) * columns] = block


def parts_of(total, group, most):
    return max(n for n in range(group, most + 1, group) if total % n == 0)


def fine_in_kernel(
    child_hbm, block_hbm, fine_hbm, w_hbm, turned_hbm, pooled_ref,
    fine_ref, child_ref, block_ref, w_ref, pool, weights, turned, tops, meta, fine_sems, turned_sems, sems, *, total, padded
):
    _, width, voxels = fine_ref.shape
    depth = w_ref.shape[1]
    group = turned.shape[1] // width
    cells = voxels // SUBS
    chunk = total // fine_sems.shape[0]
    sets = chunk // group

    def fetch(i):
        part = pl.ds(i * chunk, chunk)
        return pltpu.make_async_copy(fine_hbm.at[part], fine_ref.at[part], fine_sems.at[i])

    def store(low, high):
        part = pl.ds(low * sets * cells, (high - low) * sets * cells)
        return pltpu.make_async_copy(turned.at[part], turned_hbm.at[part], turned_sems.at[low])

    fetch(0).start(priority=1)
    small = [
        pltpu.make_async_copy(source, target, sems.at[i])
        for i, (source, target) in enumerate(
            ((w_hbm, w_ref), (child_hbm, child_ref), (block_hbm, block_ref))
        )
    ]
    for copy in small:
        copy.start()
    for i in range(1, total // chunk):
        fetch(i).start(priority=1)

    hit = hidden_voxel(iota((voxels, cells), 0)) == iota((voxels, cells), 1)
    pool[...] = jnp.where(hit, 1.0 / SUBS, 0.0).astype(BF16)
    for copy in small:
        copy.wait()
    repeat_blocks(weights, w_ref[...])
    meta[...] = jnp.full_like(meta, -1.0)
    meta[0:1, 0:total] = (child_ref[...] >> 3).astype(F32)
    meta[1:2, 0:total] = (child_ref[...] & 7).astype(F32)
    meta[2:3, 0 : block_ref.shape[1]] = block_ref[...].astype(F32)
    pooled_ref[SUBS * padded : SUBS * padded + META, :] = meta[...].astype(BF16)

    runs = run_bounds(total // chunk)
    for low, high in runs:
        for i in range(low, high):
            fetch(i).wait()
        cube = fine_ref[low * chunk : high * chunk].reshape((high - low) * chunk * width, voxels)
        octants = dot(cube, pool[...]).astype(BF16)
        for g in range((high - low) * sets):
            at = (low * sets + g) * cells
            turned[at : at + cells, :] = octants[g * group * width : (g + 1) * group * width].T
        store(low, high).start()
    for low, high in runs:
        rows = turned[low * sets * cells : high * sets * cells, :]
        hidden = jnp.maximum(dot(rows, weights[...]), 0.0).astype(BF16)
        cubes = hidden.astype(F32).reshape((high - low) * sets, SUBS, SUBS, group * depth)
        top = jnp.sum(cubes, axis=1) * (1.0 / SUBS)
        for g in range((high - low) * sets):
            for s in range(group):
                at = (low * chunk + g * group + s) * SUBS
                tops[at : at + SUBS, :] = top[g, :, s * depth : (s + 1) * depth]
    if padded != total:
        tops[total * SUBS :, :] = jnp.zeros(((padded - total) * SUBS, depth), F32)
    for v in range(SUBS):
        pooled_ref[v * padded : (v + 1) * padded, :] = tops[pl.ds(v, padded, stride=SUBS), :].astype(BF16)
    for low, high in runs:
        store(low, high).wait()


def fine_in(fine_feats, fine_child, parent_block, w_parent, padded):
    total, width, voxels = fine_feats.shape
    depth = w_parent.shape[1]
    pairs = parent_block.shape[0]
    group = 256 // width
    cells = voxels // SUBS
    chunk = parts_of(total, group, 16)
    return pl.pallas_call(
        functools.partial(fine_in_kernel, total=total, padded=padded),
        in_specs=[ANY] * 4,
        out_specs=[ANY, VMEM],
        out_shape=[
            jax.ShapeDtypeStruct((total // group * cells, group * width), BF16),
            jax.ShapeDtypeStruct((SUBS * padded + META, depth), BF16),
        ],
        scratch_shapes=[
            pltpu.VMEM(fine_feats.shape, BF16),
            pltpu.VMEM((1, total), jnp.int32),
            pltpu.VMEM((1, pairs), jnp.int32),
            pltpu.VMEM(w_parent.shape, BF16),
            pltpu.VMEM((voxels, cells), BF16),
            pltpu.VMEM((group * width, group * depth), BF16),
            pltpu.VMEM((total // group * cells, group * width), BF16),
            pltpu.VMEM((padded * SUBS, depth), F32),
            pltpu.VMEM((META, 128), F32),
            pltpu.SemaphoreType.DMA((total // chunk,)),
            pltpu.SemaphoreType.DMA((total // chunk,)),
            pltpu.SemaphoreType.DMA((3,)),
        ],
        compiler_params=params(58),
        cost_estimate=cost(total * width * voxels * 256, 2 * total * width * voxels),
        name="fine_in",
    )(fine_child[None], parent_block[None], fine_feats, w_parent)


def hide_kernel(turned_ref, w_ref, hidden_ref, weights):
    repeat_blocks(weights, w_ref[...])
    hidden_ref[...] = jnp.maximum(dot(turned_ref[...], weights[...]), 0.0).astype(BF16)


def hide(turned, w_parent):
    width, depth = w_parent.shape
    rows, wide = turned.shape
    return pl.pallas_call(
        hide_kernel,
        in_specs=[VMEM] * 2,
        out_specs=VMEM,
        out_shape=jax.ShapeDtypeStruct((rows, wide // width * depth), BF16),
        scratch_shapes=[pltpu.VMEM((wide, wide // width * depth), BF16)],
        compiler_params=params(12),
        cost_estimate=cost(rows * wide * 512, rows * wide * 6),
        name="hide",
    )(turned, w_parent)


def fold_kernel(w_ref, in_ref, out_ref):
    share = w_ref.shape[3]
    depth = in_ref.shape[0]
    nothing = jnp.zeros((share, w_ref.shape[4]), BF16)
    out_ref[:, 0, :, 2 * share :] = jnp.zeros((3, 4 * depth, 2 * share), BF16)
    out_ref[:, 3, :, 0 : 2 * share] = jnp.zeros((3, 4 * depth, 2 * share), BF16)
    for a in range(3):
        for b in range(3):
            for j in range(4):
                first = w_ref[a, b, j] if j < 3 else nothing
                second = w_ref[a, b, j - 1] if j > 0 else nothing
                pair = jnp.concatenate([first, second], axis=0)
                folded = dot_nt(in_ref[...], pair).astype(BF16)
                rows = slice(j * depth, (j + 1) * depth)
                out_ref[a, b, rows, 0 : 2 * share] = folded
                out_ref[a, b + 1, rows, 2 * share : 4 * share] = folded


def fold(w_root, w_root_in):
    share = w_root.shape[0]
    depth = w_root_in.shape[0]
    return pl.pallas_call(
        fold_kernel,
        in_specs=[VMEM, VMEM],
        out_specs=VMEM,
        out_shape=jax.ShapeDtypeStruct((3, 4, 4 * depth, 4 * share), BF16),
        compiler_params=params(16),
        cost_estimate=cost(36 * depth * 256 * 128, 6 << 20),
        name="fold",
    )(w_root.transpose(2, 3, 4, 0, 1), w_root_in)


def y_window(j):
    return ((1, 0), (0, OCT), (1, OCT), (0, 2 * OCT))[j]


def place_kernel(offsets, padded, pairs, *refs):
    groups = len(offsets)
    pooled_refs, w_ref = refs[:groups], refs[groups]
    grid_ref, place_ref, pair_ref, step_ref = refs[groups + 1 : groups + 5]
    table = refs[groups + 5]
    depth = pooled_refs[0].shape[1]
    lane_count = groups * 128
    me = lax.axis_index("ga")
    row = lax.axis_index("row")

    metas = [r[SUBS * padded : SUBS * padded + META, :] for r in pooled_refs]
    parent = jnp.concatenate([m[0:1].astype(F32) for m in metas], axis=1).astype(jnp.int32)
    octant = jnp.concatenate([m[1:2].astype(F32) for m in metas], axis=1).astype(jnp.int32)
    found = jnp.zeros((META, lane_count), F32)
    for k, offset in enumerate(offsets):
        at = iota((128, lane_count), 0)
        hot = (at < pairs) & (parent == at + (me ^ offset) * pairs)
        found += dot(metas[k], jnp.where(hot, 1.0, 0.0).astype(BF16))
    block = found[2:3].astype(jnp.int32)
    side = RXY // HALF
    z = block // (side * side) * 2 + (octant >> 2)
    y = block // side % side * 2 + (octant >> 1) % 2
    x = block % side * 2 + octant % 2
    live = parent >= 0
    place = jnp.where(live, (z * OCT + y) * OCT + x, -1)
    place_ref[...] = jnp.broadcast_to(place, place_ref.shape)

    for k, pooled_ref in enumerate(pooled_refs):
        for v in range(SUBS):
            vz, vy, vx = v >> 2, v >> 1 & 1, v & 1
            lanes = slice((vx * 4 + vz * 2 + vy) * depth, (vx * 4 + vz * 2 + vy + 1) * depth)
            table[k * 128 : k * 128 + padded, lanes] = pooled_ref[v * padded : (v + 1) * padded, :]
            if padded < 128:
                table[k * 128 + padded : (k + 1) * 128, lanes] = jnp.zeros((128 - padded, depth), BF16)

    grid_ref[:, :, 0:OCT, :] = jnp.zeros((2, RZ_REG, OCT, 4 * depth), BF16)
    grid_ref[:, :, OCT + PLANE :, :] = jnp.zeros((2, RZ_REG, OCT, 4 * depth), BF16)
    shifted = (
        (0, 1, jnp.where(live & (x < OCT - 1), place + 1, -1)),
        (1, 0, place),
        (2, 1, place),
        (3, 0, jnp.where(live & (x > 0), place - 1, -1)),
    )
    for j, vx, at in shifted:
        hot = jnp.where(iota((LAYERS * PLANE, lane_count), 0) == at, 1.0, 0.0).astype(BF16)
        for vz in range(2):
            first = (vx * 4 + vz * 2) * depth
            both = dot(hot, table[:, first : first + 2 * depth]).astype(BF16)
            for vy in range(2):
                for layer in range(LAYERS):
                    grid_ref[vy, layer * 2 + vz, OCT : OCT + PLANE, j * depth : (j + 1) * depth] = both[
                        layer * PLANE : (layer + 1) * PLANE, vy * depth : (vy + 1) * depth
                    ]

    even = row % 2 == 0
    for out_ref, up in ((pair_ref, even), (step_ref, jnp.logical_not(even))):
        plane = jnp.where(up, RZ_REG - 1, 0)
        dz = jnp.where(up, 0, 2)
        total = None
        for j in range(4):
            vy, first = y_window(j)
            part = dot(grid_ref[vy, plane, first : first + PLANE, :], w_ref[dz, j])
            total = part if total is None else total + part
        out_ref[...] = total.astype(BF16)


def place(pooled, offsets, folded, padded, pairs):
    groups = len(offsets)
    depth = pooled[0].shape[1]
    wide = folded.shape[3]
    return pl.pallas_call(
        functools.partial(place_kernel, offsets, padded, pairs),
        in_specs=[VMEM] * (groups + 1),
        out_specs=[VMEM] * 4,
        out_shape=[
            jax.ShapeDtypeStruct((2, RZ_REG, BORDERED, 4 * depth), BF16),
            jax.ShapeDtypeStruct((8, groups * 128), jnp.int32),
            jax.ShapeDtypeStruct((PLANE, wide), BF16),
            jax.ShapeDtypeStruct((PLANE, wide), BF16),
        ],
        scratch_shapes=[pltpu.VMEM((groups * 128, SUBS * depth), BF16)],
        compiler_params=params(24),
        cost_estimate=cost(2 << 28, 6 << 20),
        name="place",
    )(*pooled, folded)


def conv_kernel(grid_ref, w_ref, out_ref):
    for z in range(RZ_REG):
        total = None
        for a in range(3):
            if not 0 <= z + a - 1 < RZ_REG:
                continue
            for j in range(4):
                vy, first = y_window(j)
                part = dot(grid_ref[vy, z + a - 1, first : first + PLANE, :], w_ref[a, j])
                total = part if total is None else total + part
        out_ref[z] = total


def conv(grid, folded):
    wide = folded.shape[3]
    return pl.pallas_call(
        conv_kernel,
        in_specs=[VMEM, VMEM],
        out_specs=VMEM,
        out_shape=jax.ShapeDtypeStruct((RZ_REG, PLANE, wide), F32),
        compiler_params=params(16),
        cost_estimate=cost(10 * 4 * PLANE * 512 * 256, 6 << 20),
        name="conv",
    )(grid, folded)


def finish_kernel(padded, order, place_ref, sums_ref, pair_ref, step_ref, bias_ref, *refs):
    root_ref, empty_ref, send_refs = refs[0], refs[1], refs[2:]
    lane_count = place_ref.shape[1]
    row = lax.axis_index("row")
    even = row % 2 == 0
    last = lax.axis_size("row") - 1
    bias = jnp.concatenate([bias_ref[...]] * 4, axis=1)
    pair = pair_ref[...].astype(F32)
    step = step_ref[...].astype(F32)
    above = jnp.where(even, pair, step)
    below = jnp.where(even, step, pair)
    above = jnp.where(row < last, above, 0.0)
    below = jnp.where(row > 0, below, 0.0)
    column = place_ref[...].astype(F32).T[:, 0:1].astype(jnp.int32)
    empty_ref[...] = jnp.broadcast_to(jnp.where(column[0:padded] < 0, -1e30, 0.0), empty_ref.shape)
    hot = jnp.where(column == iota((lane_count, LAYERS * PLANE), 1), 1.0, 0.0).astype(BF16)
    for z in range(RZ_REG):
        total = sums_ref[z] + bias
        if z == 0:
            total += below
        if z == RZ_REG - 1:
            total += above
        root_ref[z % 2, z // 2 * PLANE : (z // 2 + 1) * PLANE, :] = jnp.maximum(total, 0.0).astype(BF16)
    wide = root_ref.shape[2]
    for vz in range(2):
        picked = dot(hot, root_ref[vz]).astype(BF16)
        for send_ref, k in zip(send_refs, order):
            send_ref[:, vz * wide : (vz + 1) * wide] = picked[k * 128 : k * 128 + padded]


def finish(places, sums, pair, step, root_bias, order, padded):
    wide = sums.shape[2]
    groups = len(order)
    return pl.pallas_call(
        functools.partial(finish_kernel, padded, order),
        in_specs=[VMEM] * 5,
        out_specs=[VMEM] * (groups + 2),
        out_shape=[
            jax.ShapeDtypeStruct((2, LAYERS * PLANE, wide), BF16),
            jax.ShapeDtypeStruct((padded, 128), F32),
        ]
        + [jax.ShapeDtypeStruct((padded, 2 * wide), BF16)] * groups,
        compiler_params=params(24),
        cost_estimate=cost(1 << 27, 3 << 20),
        name="finish",
    )(places, sums, pair, step, root_bias[None])


def unravel_kernel(offsets, root_ref, down_ref, skip_ref, out_ref, lift_ref, weights_ref, spread_ref):
    share = root_ref.shape[2] // 4
    rows, half = PLANE, PLANE // 2
    x, y = iota((rows, half), 0), iota((rows, half), 1)
    same = x // RXY == y // OCT
    spread = [
        jnp.where(same & (x % RXY == 2 * (y % OCT) + vx), 1.0, 0.0).astype(BF16) for vx in range(2)
    ]
    lines = half // OCT
    for z in range(RZ_REG):
        for part in range(2):
            first = z // 2 * PLANE + part * half
            for vy in range(2):
                at = vy * 2 * share
                even = root_ref[z % 2, first : first + half, at : at + share]
                odd = root_ref[z % 2, first : first + half, at + share : at + 2 * share]
                line = (dot(spread[0], even) + dot(spread[1], odd)).astype(BF16)
                out_ref[z, part * lines : (part + 1) * lines, vy] = line.reshape(lines, RXY, share)

    me = lax.axis_index("ga")
    width, depth = skip_ref.shape
    lift_ref[...] = jnp.zeros_like(lift_ref)
    for k, offset in enumerate(offsets):
        own = down_ref[pl.ds(pl.multiple_of((me ^ offset) * share, share), share), :]
        for vx in range(2):
            first = (k * 2 + vx) * share
            lift_ref[first : first + share, vx * depth : (vx + 1) * depth] = own
    repeat_blocks(weights_ref, skip_ref[...].T)
    hit = hidden_voxel(iota(spread_ref.shape, 1)) == iota(spread_ref.shape, 0)
    spread_ref[...] = jnp.where(hit, 1.0, 0.0).astype(BF16)


def unravel(root, w_down, w_skip, offsets, voxels):
    share = root.shape[2] // 4
    depth, width = w_skip.shape
    group = 256 // width
    out, lift, weights, spread = pl.pallas_call(
        functools.partial(unravel_kernel, offsets),
        in_specs=[VMEM] * 3,
        out_specs=[VMEM] * 4,
        out_shape=[
            jax.ShapeDtypeStruct((RZ_REG, OCT, 2, RXY, share), BF16),
            jax.ShapeDtypeStruct((len(offsets) * 2 * share, 2 * depth), BF16),
            jax.ShapeDtypeStruct((group * depth, group * width), BF16),
            jax.ShapeDtypeStruct((voxels // SUBS, voxels), BF16),
        ],
        compiler_params=params(12),
        cost_estimate=cost(1 << 28, 2 << 20),
        name="unravel",
    )(root, w_down, w_skip.T)
    return out.reshape(RZ_REG, RXY, RXY, share).transpose(3, 0, 1, 2), lift, weights, spread


def fine_out_kernel(groups, *refs):
    fine_ref, hidden_ref, empty_ref, lift_ref, weights_ref, spread_ref = refs[:6]
    come_refs = refs[6 : 6 + groups]
    out_hbm, out_ref, lifted, skips, sems = refs[6 + groups :]
    total, width, voxels = fine_ref.shape
    depth = lift_ref.shape[1] // 2
    group = hidden_ref.shape[1] // depth
    cells = voxels // SUBS
    share = come_refs[0].shape[1] // SUBS
    chunk = total // sems.shape[0]
    sets = chunk // group

    for zy in range(4):
        lanes = slice(zy * 2 * share, (zy + 1) * 2 * share)
        both = dot(jnp.concatenate([r[:, lanes] for r in come_refs], axis=1), lift_ref[...])
        slots = both.shape[0]
        for vx in range(2):
            top = both[:, vx * depth : (vx + 1) * depth] + empty_ref[...]
            lifted[pl.ds(zy * 2 + vx, slots, stride=SUBS), :] = top

    for i in range(total // chunk):
        rows = []
        for g in range(sets):
            at = i * sets + g
            tops = [
                lifted[(at * group + s) * SUBS : (at * group + s + 1) * SUBS, :] for s in range(group)
            ]
            hidden = hidden_ref[at * cells : (at + 1) * cells, :].astype(F32).reshape(SUBS, SUBS, group * depth)
            decoded = jnp.maximum(hidden + jnp.concatenate(tops, axis=1)[None], 0.0)
            rows.append(decoded.reshape(cells, group * depth).astype(BF16))
        skip = dot(jnp.concatenate(rows, axis=0), weights_ref[...]).astype(BF16)
        for g in range(sets):
            at = (i * sets + g) * group * width
            skips[at : at + group * width, :] = skip[g * cells : (g + 1) * cells].T

    def send(i):
        part = pl.ds(i * chunk, chunk)
        return pltpu.make_async_copy(out_ref.at[part], out_hbm.at[part], sems.at[i])

    for i in range(total // chunk):
        part = slice(i * chunk, (i + 1) * chunk)
        up = dot(skips[i * chunk * width : (i + 1) * chunk * width, :], spread_ref[...])
        cube = fine_ref[part].reshape(chunk * width, voxels)
        out_ref[part] = (cube.astype(F32) + up).astype(BF16).reshape(chunk, width, voxels)
        send(i).start()
    for i in range(total // chunk):
        send(i).wait()


def fine_out(fine_feats, hidden, empty, lift, weights, spread, come):
    total, width, voxels = fine_feats.shape
    padded = empty.shape[0]
    depth = lift.shape[1] // 2
    group = 256 // width
    groups = len(come)
    chunk = parts_of(total, group, 16)
    return pl.pallas_call(
        functools.partial(fine_out_kernel, groups),
        in_specs=[VMEM] * (6 + groups),
        out_specs=ANY,
        out_shape=jax.ShapeDtypeStruct(fine_feats.shape, BF16),
        scratch_shapes=[
            pltpu.VMEM(fine_feats.shape, BF16),
            pltpu.VMEM((padded * SUBS, depth), F32),
            pltpu.VMEM((total * width, voxels // SUBS), BF16),
            pltpu.SemaphoreType.DMA((total // chunk,)),
        ],
        compiler_params=params(28),
        cost_estimate=cost(total * width * voxels * 256, 4 * total * width * voxels),
        name="fine_out",
    )(fine_feats, hidden, empty, lift, weights, spread, *come)


def shards(
    fine_feats, fine_child, parent_block, w_parent, w_root_in, w_root, root_bias, w_down, w_skip
):
    groups = lax.axis_size("ga")
    rows = lax.axis_size("row")
    slots = fine_feats.shape[0]
    padded = -(-slots // META) * META
    pairs = parent_block.shape[0]

    turned, pooled = fine_in(fine_feats, fine_child, parent_block, w_parent, padded)

    hidden = hide(turned, w_parent)
    folded = fold(w_root, w_root_in)

    gathered, offsets = [pooled], [0]
    bit = groups // 2
    while bit:
        swap = [(i, i ^ bit) for i in range(groups)]
        gathered += [lax.ppermute(part, "ga", swap) for part in gathered]
        offsets += [offset ^ bit for offset in offsets]
        if bit == groups // 2:
            gathered[1], folded, hidden = lax.optimization_barrier((gathered[1], folded, hidden))
        bit //= 2
    offsets = tuple(offsets)

    grid, places, pair, step = place(gathered, offsets, folded, padded, pairs)
    pair_swap = [(i, i ^ 1) for i in range(rows) if i ^ 1 < rows]
    step_swap = []
    for i in range(rows):
        inner = 0 < i < rows - 1
        for j in range(groups):
            target = ((i - 1 ^ 1) + 1) * groups + j if inner else i * groups + (j ^ 1)
            step_swap.append((i * groups + j, target))
    pair = lax.ppermute(pair, "row", pair_swap)
    step = lax.ppermute(step, ("row", "ga"), step_swap)
    sums = conv(grid, folded)
    order = sorted(range(groups), key=lambda k: (offsets[k] > 0, offsets[k] < groups // 2, offsets[k]))
    root, empty, *sends = finish(places, sums, pair, step, root_bias, order, padded)
    come = sends[:1]
    for k, send in zip(order[1:], sends[1:]):
        come.append(lax.ppermute(send, "ga", [(i, i ^ offsets[k]) for i in range(groups)]))
    root_out, lift, weights, spread = unravel(
        root, w_down, w_skip, [offsets[k] for k in order], fine_feats.shape[2]
    )
    fine = fine_out(fine_feats, hidden, empty, lift, weights, spread, come)
    return (fine, root_out)


def solution(mesh):
    return jax.shard_map(
        shards,
        mesh=mesh,
        in_specs=(
            P(("row", "ga"), None, None),
            P(("row", "ga")),
            P(("row", "ga")),
            P(),
            P(),
            P("ga", None, None, None, None),
            P("ga"),
            P(),
            P(),
        ),
        out_specs=(P(("row", "ga"), None, None), P("ga", "row", None, None)),
        check_vma=False,
    )
```

```python
import functools

import jax
import jax.numpy as jnp
from jax import lax
from jax.experimental import pallas as pl
from jax.experimental.pallas import tpu as pltpu
from jax.sharding import PartitionSpec as P

B = 8
RXY = 32
RZ_REG = 4

HALF = B // 2
OCT = RXY // 2
LAYERS = RZ_REG // 2
PLANE = OCT * OCT
INNER = (1, 2)
OUTER = (0, 3)
BORDERED = PLANE + 2 * OCT
SUBS = 8
META = 16
BF16 = jnp.bfloat16
F32 = jnp.float32
VMEM = pl.BlockSpec(memory_space=pltpu.VMEM)
ANY = pl.BlockSpec(memory_space=pl.ANY)


def params(mib):
    return pltpu.CompilerParams(vmem_limit_bytes=mib << 20)


def cost(macs, moved):
    return pl.CostEstimate(flops=2 * macs, bytes_accessed=moved, transcendentals=0)


def iota(shape, axis):
    return lax.broadcasted_iota(jnp.int32, shape, axis)


def dot(left, right):
    return jnp.dot(left, right, preferred_element_type=F32)


def dot_nt(left, right):
    return lax.dot_general(left, right, (((1,), (1,)), ((), ())), preferred_element_type=F32)


def hidden_voxel(fine):
    edge = B.bit_length() - 1
    z, y, x = fine >> 2 * edge, fine >> edge & B - 1, fine & B - 1
    low = (z >> 1 & 1) * 4 + (y >> 1 & 1) * 2 + (x >> 1 & 1)
    high = (z >> edge - 1) * 4 + (y >> edge - 1) * 2 + (x >> edge - 1)
    return low * SUBS + high


def run_bounds(count):
    cuts = [0]
    while cuts[-1] < count:
        cuts.append(min(2 * cuts[-1] + 1, count))
    return list(zip(cuts, cuts[1:]))


def repeat_blocks(ref, block):
    rows, columns = block.shape
    ref[...] = jnp.zeros_like(ref)
    for s in range(ref.shape[0] // rows):
        ref[s * rows : (s + 1) * rows, s * columns : (s + 1) * columns] = block


def parts_of(total, group, most):
    return max(n for n in range(group, most + 1, group) if total % n == 0)


def fine_in_kernel(
    child_hbm, block_hbm, fine_hbm, w_hbm, turned_hbm, pooled_ref,
    fine_ref, child_ref, block_ref, w_ref, pool, weights, turned, tops, meta, fine_sems, turned_sems, sems, *, total, padded
):
    _, width, voxels = fine_ref.shape
    depth = w_ref.shape[1]
    group = turned.shape[1] // width
    cells = voxels // SUBS
    chunk = total // fine_sems.shape[0]
    sets = chunk // group

    def fetch(i):
        part = pl.ds(i * chunk, chunk)
        return pltpu.make_async_copy(fine_hbm.at[part], fine_ref.at[part], fine_sems.at[i])

    def store(low, high):
        part = pl.ds(low * sets * cells, (high - low) * sets * cells)
        return pltpu.make_async_copy(turned.at[part], turned_hbm.at[part], turned_sems.at[low])

    fetch(0).start(priority=1)
    small = [
        pltpu.make_async_copy(source, target, sems.at[i])
        for i, (source, target) in enumerate(
            ((w_hbm, w_ref), (child_hbm, child_ref), (block_hbm, block_ref))
        )
    ]
    for copy in small:
        copy.start()
    for i in range(1, total // chunk):
        fetch(i).start(priority=1)

    hit = hidden_voxel(iota((voxels, cells), 0)) == iota((voxels, cells), 1)
    pool[...] = jnp.where(hit, 1.0 / SUBS, 0.0).astype(BF16)
    for copy in small:
        copy.wait()
    repeat_blocks(weights, w_ref[...])
    meta[...] = jnp.full_like(meta, -1.0)
    meta[0:1, 0:total] = (child_ref[...] >> 3).astype(F32)
    meta[1:2, 0:total] = (child_ref[...] & 7).astype(F32)
    meta[2:3, 0 : block_ref.shape[1]] = block_ref[...].astype(F32)
    pooled_ref[SUBS * padded : SUBS * padded + META, :] = meta[...].astype(BF16)

    runs = run_bounds(total // chunk)
    for low, high in runs:
        for i in range(low, high):
            fetch(i).wait()
        cube = fine_ref[low * chunk : high * chunk].reshape((high - low) * chunk * width, voxels)
        octants = dot(cube, pool[...]).astype(BF16)
        for g in range((high - low) * sets):
            at = (low * sets + g) * cells
            turned[at : at + cells, :] = octants[g * group * width : (g + 1) * group * width].T
        store(low, high).start()
    for low, high in runs:
        rows = turned[low * sets * cells : high * sets * cells, :]
        hidden = jnp.maximum(dot(rows, weights[...]), 0.0).astype(BF16)
        cubes = hidden.astype(F32).reshape((high - low) * sets, SUBS, SUBS, group * depth)
        top = jnp.sum(cubes, axis=1) * (1.0 / SUBS)
        for g in range((high - low) * sets):
            for s in range(group):
                at = (low * chunk + g * group + s) * SUBS
                tops[at : at + SUBS, :] = top[g, :, s * depth : (s + 1) * depth]
    if padded != total:
        tops[total * SUBS :, :] = jnp.zeros(((padded - total) * SUBS, depth), F32)
    for v in range(SUBS):
        pooled_ref[v * padded : (v + 1) * padded, :] = tops[pl.ds(v, padded, stride=SUBS), :].astype(BF16)
    for low, high in runs:
        store(low, high).wait()


def fine_in(fine_feats, fine_child, parent_block, w_parent, padded):
    total, width, voxels = fine_feats.shape
    depth = w_parent.shape[1]
    pairs = parent_block.shape[0]
    group = 256 // width
    cells = voxels // SUBS
    chunk = parts_of(total, group, 16)
    return pl.pallas_call(
        functools.partial(fine_in_kernel, total=total, padded=padded),
        in_specs=[ANY] * 4,
        out_specs=[ANY, VMEM],
        out_shape=[
            jax.ShapeDtypeStruct((total // group * cells, group * width), BF16),
            jax.ShapeDtypeStruct((SUBS * padded + META, depth), BF16),
        ],
        scratch_shapes=[
            pltpu.VMEM(fine_feats.shape, BF16),
            pltpu.VMEM((1, total), jnp.int32),
            pltpu.VMEM((1, pairs), jnp.int32),
            pltpu.VMEM(w_parent.shape, BF16),
            pltpu.VMEM((voxels, cells), BF16),
            pltpu.VMEM((group * width, group * depth), BF16),
            pltpu.VMEM((total // group * cells, group * width), BF16),
            pltpu.VMEM((padded * SUBS, depth), F32),
            pltpu.VMEM((META, 128), F32),
            pltpu.SemaphoreType.DMA((total // chunk,)),
            pltpu.SemaphoreType.DMA((total // chunk,)),
            pltpu.SemaphoreType.DMA((3,)),
        ],
        compiler_params=params(58),
        cost_estimate=cost(total * width * voxels * 256, 2 * total * width * voxels),
        name="fine_in",
    )(fine_child[None], parent_block[None], fine_feats, w_parent)


def hide_kernel(turned_ref, w_ref, hidden_ref, weights):
    repeat_blocks(weights, w_ref[...])
    hidden_ref[...] = jnp.maximum(dot(turned_ref[...], weights[...]), 0.0).astype(BF16)


def hide(turned, w_parent):
    width, depth = w_parent.shape
    rows, wide = turned.shape
    return pl.pallas_call(
        hide_kernel,
        in_specs=[VMEM] * 2,
        out_specs=VMEM,
        out_shape=jax.ShapeDtypeStruct((rows, wide // width * depth), BF16),
        scratch_shapes=[pltpu.VMEM((wide, wide // width * depth), BF16)],
        compiler_params=params(12),
        cost_estimate=cost(rows * wide * 512, rows * wide * 6),
        name="hide",
    )(turned, w_parent)


def fold_kernel(w_ref, in_ref, out_ref):
    share = w_ref.shape[3]
    depth = in_ref.shape[0]
    nothing = jnp.zeros((share, w_ref.shape[4]), BF16)
    out_ref[:, 0, :, 2 * share :] = jnp.zeros((3, 4 * depth, 2 * share), BF16)
    out_ref[:, 3, :, 0 : 2 * share] = jnp.zeros((3, 4 * depth, 2 * share), BF16)
    for a in range(3):
        for b in range(3):
            for j in range(4):
                first = w_ref[a, b, j] if j < 3 else nothing
                second = w_ref[a, b, j - 1] if j > 0 else nothing
                pair = jnp.concatenate([first, second], axis=0)
                folded = dot_nt(in_ref[...], pair).astype(BF16)
                rows = slice(j * depth, (j + 1) * depth)
                out_ref[a, b, rows, 0 : 2 * share] = folded
                out_ref[a, b + 1, rows, 2 * share : 4 * share] = folded


def fold(w_root, w_root_in):
    share = w_root.shape[0]
    depth = w_root_in.shape[0]
    return pl.pallas_call(
        fold_kernel,
        in_specs=[VMEM, VMEM],
        out_specs=VMEM,
        out_shape=jax.ShapeDtypeStruct((3, 4, 4 * depth, 4 * share), BF16),
        compiler_params=params(16),
        cost_estimate=cost(36 * depth * 256 * 128, 6 << 20),
        name="fold",
    )(w_root.transpose(2, 3, 4, 0, 1), w_root_in)


def y_window(j):
    return ((1, 0), (0, OCT), (1, OCT), (0, 2 * OCT))[j]


def fill_planes(planes_ref, planes, place, table):
    depth = table.shape[1] // SUBS
    x = place % OCT
    planes_ref[:, :, 0:OCT, :] = jnp.zeros((2, LAYERS, OCT, 4 * depth), BF16)
    planes_ref[:, :, OCT + PLANE :, :] = jnp.zeros((2, LAYERS, OCT, 4 * depth), BF16)
    live = place >= 0
    shifted = (
        (0, 1, jnp.where(live & (x < OCT - 1), place + 1, -1)),
        (1, 0, place),
        (2, 1, place),
        (3, 0, jnp.where(live & (x > 0), place - 1, -1)),
    )
    for j, vx, at in shifted:
        hot = jnp.where(iota((LAYERS * PLANE, place.shape[1]), 0) == at, 1.0, 0.0).astype(BF16)
        for layer, z in enumerate(planes):
            first = (vx * 4 + z % 2 * 2) * depth
            both = dot(hot[layer * PLANE : (layer + 1) * PLANE], table[:, first : first + 2 * depth]).astype(BF16)
            for vy in range(2):
                planes_ref[vy, layer, OCT : OCT + PLANE, j * depth : (j + 1) * depth] = both[
                    :, vy * depth : (vy + 1) * depth
                ]


def place_kernel(offsets, padded, pairs, *refs):
    groups = len(offsets)
    pooled_refs, w_ref = refs[:groups], refs[groups]
    faces_ref, table, place_ref, pair_ref, step_ref = refs[groups + 1 : groups + 6]
    depth = pooled_refs[0].shape[1]
    lane_count = groups * 128
    me = lax.axis_index("ga")
    row = lax.axis_index("row")

    metas = [r[SUBS * padded : SUBS * padded + META, :] for r in pooled_refs]
    parent = jnp.concatenate([m[0:1].astype(F32) for m in metas], axis=1).astype(jnp.int32)
    octant = jnp.concatenate([m[1:2].astype(F32) for m in metas], axis=1).astype(jnp.int32)
    found = jnp.zeros((META, lane_count), F32)
    for k, offset in enumerate(offsets):
        at = iota((128, lane_count), 0)
        hot = (at < pairs) & (parent == at + (me ^ offset) * pairs)
        found += dot(metas[k], jnp.where(hot, 1.0, 0.0).astype(BF16))
    block = found[2:3].astype(jnp.int32)
    side = RXY // HALF
    z = block // (side * side) * 2 + (octant >> 2)
    y = block // side % side * 2 + (octant >> 1) % 2
    x = block % side * 2 + octant % 2
    live = parent >= 0
    place = jnp.where(live, (z * OCT + y) * OCT + x, -1)
    place_ref[...] = jnp.broadcast_to(place, place_ref.shape)

    for k, pooled_ref in enumerate(pooled_refs):
        for v in range(SUBS):
            vz, vy, vx = v >> 2, v >> 1 & 1, v & 1
            lanes = slice((vx * 4 + vz * 2 + vy) * depth, (vx * 4 + vz * 2 + vy + 1) * depth)
            table[k * 128 : k * 128 + padded, lanes] = pooled_ref[v * padded : (v + 1) * padded, :]
            if padded < 128:
                table[k * 128 + padded : (k + 1) * 128, lanes] = jnp.zeros((128 - padded, depth), BF16)

    fill_planes(faces_ref, OUTER, place, table)

    even = row % 2 == 0
    for out_ref, up in ((pair_ref, even), (step_ref, jnp.logical_not(even))):
        plane = jnp.where(up, 1, 0)
        dz = jnp.where(up, 0, 2)
        total = None
        for j in range(4):
            vy, first = y_window(j)
            part = dot(faces_ref[vy, plane, first : first + PLANE, :], w_ref[dz, j])
            total = part if total is None else total + part
        out_ref[...] = total.astype(BF16)


def place(pooled, offsets, folded, padded, pairs):
    groups = len(offsets)
    depth = pooled[0].shape[1]
    wide = folded.shape[3]
    return pl.pallas_call(
        functools.partial(place_kernel, offsets, padded, pairs),
        in_specs=[VMEM] * (groups + 1),
        out_specs=[VMEM] * 5,
        out_shape=[
            jax.ShapeDtypeStruct((2, LAYERS, BORDERED, 4 * depth), BF16),
            jax.ShapeDtypeStruct((groups * 128, SUBS * depth), BF16),
            jax.ShapeDtypeStruct((8, groups * 128), jnp.int32),
            jax.ShapeDtypeStruct((PLANE, wide), BF16),
            jax.ShapeDtypeStruct((PLANE, wide), BF16),
        ],
        compiler_params=params(16),
        cost_estimate=cost(1 << 28, 6 << 20),
        name="place",
    )(*pooled, folded)


def conv_kernel(faces_ref, table_ref, place_ref, w_ref, out_ref, inside):
    fill_planes(inside, INNER, place_ref[0:1, :], table_ref)
    for z in range(RZ_REG):
        total = None
        for a in range(3):
            source = z + a - 1
            if not 0 <= source < RZ_REG:
                continue
            planes = inside if source in INNER else faces_ref
            for j in range(4):
                vy, first = y_window(j)
                part = dot(planes[vy, source // 2, first : first + PLANE, :], w_ref[a, j])
                total = part if total is None else total + part
        out_ref[z] = total


def conv(faces, table, places, folded):
    wide = folded.shape[3]
    return pl.pallas_call(
        conv_kernel,
        in_specs=[VMEM] * 4,
        out_specs=VMEM,
        out_shape=jax.ShapeDtypeStruct((RZ_REG, PLANE, wide), F32),
        scratch_shapes=[pltpu.VMEM(faces.shape, BF16)],
        compiler_params=params(20),
        cost_estimate=cost(10 * 4 * PLANE * 512 * 256, 6 << 20),
        name="conv",
    )(faces, table, places, folded)


def finish_kernel(padded, order, place_ref, sums_ref, pair_ref, step_ref, bias_ref, *refs):
    root_ref, empty_ref, send_refs = refs[0], refs[1], refs[2:]
    lane_count = place_ref.shape[1]
    row = lax.axis_index("row")
    even = row % 2 == 0
    last = lax.axis_size("row") - 1
    bias = jnp.concatenate([bias_ref[...]] * 4, axis=1)
    pair = pair_ref[...].astype(F32)
    step = step_ref[...].astype(F32)
    above = jnp.where(even, pair, step)
    below = jnp.where(even, step, pair)
    above = jnp.where(row < last, above, 0.0)
    below = jnp.where(row > 0, below, 0.0)
    column = place_ref[...].astype(F32).T[:, 0:1].astype(jnp.int32)
    empty_ref[...] = jnp.broadcast_to(jnp.where(column[0:padded] < 0, -1e30, 0.0), empty_ref.shape)
    hot = jnp.where(column == iota((lane_count, LAYERS * PLANE), 1), 1.0, 0.0).astype(BF16)
    for z in range(RZ_REG):
        total = sums_ref[z] + bias
        if z == 0:
            total += below
        if z == RZ_REG - 1:
            total += above
        root_ref[z % 2, z // 2 * PLANE : (z // 2 + 1) * PLANE, :] = jnp.maximum(total, 0.0).astype(BF16)
    wide = root_ref.shape[2]
    for vz in range(2):
        picked = dot(hot, root_ref[vz]).astype(BF16)
        for send_ref, k in zip(send_refs, order):
            send_ref[:, vz * wide : (vz + 1) * wide] = picked[k * 128 : k * 128 + padded]


def finish(places, sums, pair, step, root_bias, order, padded):
    wide = sums.shape[2]
    groups = len(order)
    return pl.pallas_call(
        functools.partial(finish_kernel, padded, order),
        in_specs=[VMEM] * 5,
        out_specs=[VMEM] * (groups + 2),
        out_shape=[
            jax.ShapeDtypeStruct((2, LAYERS * PLANE, wide), BF16),
            jax.ShapeDtypeStruct((padded, 128), F32),
        ]
        + [jax.ShapeDtypeStruct((padded, 2 * wide), BF16)] * groups,
        compiler_params=params(24),
        cost_estimate=cost(1 << 27, 3 << 20),
        name="finish",
    )(places, sums, pair, step, root_bias[None])


def unravel_kernel(offsets, root_ref, down_ref, skip_ref, out_ref, lift_ref, weights_ref, spread_ref):
    share = root_ref.shape[2] // 4
    rows, half = PLANE, PLANE // 2
    x, y = iota((rows, half), 0), iota((rows, half), 1)
    same = x // RXY == y // OCT
    spread = [
        jnp.where(same & (x % RXY == 2 * (y % OCT) + vx), 1.0, 0.0).astype(BF16) for vx in range(2)
    ]
    lines = half // OCT
    for z in range(RZ_REG):
        for part in range(2):
            first = z // 2 * PLANE + part * half
            for vy in range(2):
                at = vy * 2 * share
                even = root_ref[z % 2, first : first + half, at : at + share]
                odd = root_ref[z % 2, first : first + half, at + share : at + 2 * share]
                line = (dot(spread[0], even) + dot(spread[1], odd)).astype(BF16)
                out_ref[z, part * lines : (part + 1) * lines, vy] = line.reshape(lines, RXY, share)

    me = lax.axis_index("ga")
    width, depth = skip_ref.shape
    lift_ref[...] = jnp.zeros_like(lift_ref)
    for k, offset in enumerate(offsets):
        own = down_ref[pl.ds(pl.multiple_of((me ^ offset) * share, share), share), :]
        for vx in range(2):
            first = (k * 2 + vx) * share
            lift_ref[first : first + share, vx * depth : (vx + 1) * depth] = own
    repeat_blocks(weights_ref, skip_ref[...].T)
    hit = hidden_voxel(iota(spread_ref.shape, 1)) == iota(spread_ref.shape, 0)
    spread_ref[...] = jnp.where(hit, 1.0, 0.0).astype(BF16)


def unravel(root, w_down, w_skip, offsets, voxels):
    share = root.shape[2] // 4
    depth, width = w_skip.shape
    group = 256 // width
    out, lift, weights, spread = pl.pallas_call(
        functools.partial(unravel_kernel, offsets),
        in_specs=[VMEM] * 3,
        out_specs=[VMEM] * 4,
        out_shape=[
            jax.ShapeDtypeStruct((RZ_REG, OCT, 2, RXY, share), BF16),
            jax.ShapeDtypeStruct((len(offsets) * 2 * share, 2 * depth), BF16),
            jax.ShapeDtypeStruct((group * depth, group * width), BF16),
            jax.ShapeDtypeStruct((voxels // SUBS, voxels), BF16),
        ],
        compiler_params=params(12),
        cost_estimate=cost(1 << 28, 2 << 20),
        name="unravel",
    )(root, w_down, w_skip.T)
    return out.reshape(RZ_REG, RXY, RXY, share).transpose(3, 0, 1, 2), lift, weights, spread


def fine_out_kernel(groups, *refs):
    fine_ref, hidden_ref, empty_ref, lift_ref, weights_ref, spread_ref = refs[:6]
    come_refs = refs[6 : 6 + groups]
    out_hbm, out_ref, lifted, skips, sems = refs[6 + groups :]
    total, width, voxels = fine_ref.shape
    depth = lift_ref.shape[1] // 2
    group = hidden_ref.shape[1] // depth
    cells = voxels // SUBS
    share = come_refs[0].shape[1] // SUBS
    chunk = total // sems.shape[0]
    sets = chunk // group

    for zy in range(4):
        lanes = slice(zy * 2 * share, (zy + 1) * 2 * share)
        both = dot(jnp.concatenate([r[:, lanes] for r in come_refs], axis=1), lift_ref[...])
        slots = both.shape[0]
        for vx in range(2):
            top = both[:, vx * depth : (vx + 1) * depth] + empty_ref[...]
            lifted[pl.ds(zy * 2 + vx, slots, stride=SUBS), :] = top

    for i in range(total // chunk):
        rows = []
        for g in range(sets):
            at = i * sets + g
            tops = [
                lifted[(at * group + s) * SUBS : (at * group + s + 1) * SUBS, :] for s in range(group)
            ]
            hidden = hidden_ref[at * cells : (at + 1) * cells, :].astype(F32).reshape(SUBS, SUBS, group * depth)
            decoded = jnp.maximum(hidden + jnp.concatenate(tops, axis=1)[None], 0.0)
            rows.append(decoded.reshape(cells, group * depth).astype(BF16))
        skip = dot(jnp.concatenate(rows, axis=0), weights_ref[...]).astype(BF16)
        for g in range(sets):
            at = (i * sets + g) * group * width
            skips[at : at + group * width, :] = skip[g * cells : (g + 1) * cells].T

    def send(i):
        part = pl.ds(i * chunk, chunk)
        return pltpu.make_async_copy(out_ref.at[part], out_hbm.at[part], sems.at[i])

    for i in range(total // chunk):
        part = slice(i * chunk, (i + 1) * chunk)
        up = dot(skips[i * chunk * width : (i + 1) * chunk * width, :], spread_ref[...])
        cube = fine_ref[part].reshape(chunk * width, voxels)
        out_ref[part] = (cube.astype(F32) + up).astype(BF16).reshape(chunk, width, voxels)
        send(i).start()
    for i in range(total // chunk):
        send(i).wait()


def fine_out(fine_feats, hidden, empty, lift, weights, spread, come):
    total, width, voxels = fine_feats.shape
    padded = empty.shape[0]
    depth = lift.shape[1] // 2
    group = 256 // width
    groups = len(come)
    chunk = parts_of(total, group, 16)
    return pl.pallas_call(
        functools.partial(fine_out_kernel, groups),
        in_specs=[VMEM] * (6 + groups),
        out_specs=ANY,
        out_shape=jax.ShapeDtypeStruct(fine_feats.shape, BF16),
        scratch_shapes=[
            pltpu.VMEM(fine_feats.shape, BF16),
            pltpu.VMEM((padded * SUBS, depth), F32),
            pltpu.VMEM((total * width, voxels // SUBS), BF16),
            pltpu.SemaphoreType.DMA((total // chunk,)),
        ],
        compiler_params=params(28),
        cost_estimate=cost(total * width * voxels * 256, 4 * total * width * voxels),
        name="fine_out",
    )(fine_feats, hidden, empty, lift, weights, spread, *come)


def shards(
    fine_feats, fine_child, parent_block, w_parent, w_root_in, w_root, root_bias, w_down, w_skip
):
    groups = lax.axis_size("ga")
    rows = lax.axis_size("row")
    slots = fine_feats.shape[0]
    padded = -(-slots // META) * META
    pairs = parent_block.shape[0]

    turned, pooled = fine_in(fine_feats, fine_child, parent_block, w_parent, padded)

    hidden = hide(turned, w_parent)
    folded = fold(w_root, w_root_in)

    gathered, offsets = [pooled], [0]
    bit = groups // 2
    while bit:
        swap = [(i, i ^ bit) for i in range(groups)]
        gathered += [lax.ppermute(part, "ga", swap) for part in gathered]
        offsets += [offset ^ bit for offset in offsets]
        if bit == groups // 2:
            gathered[1], folded, hidden = lax.optimization_barrier((gathered[1], folded, hidden))
        bit //= 2
    offsets = tuple(offsets)

    faces, table, places, pair, step = place(gathered, offsets, folded, padded, pairs)
    pair_swap = [(i, i ^ 1) for i in range(rows) if i ^ 1 < rows]
    step_swap = []
    for i in range(rows):
        inner = 0 < i < rows - 1
        for j in range(groups):
            target = ((i - 1 ^ 1) + 1) * groups + j if inner else i * groups + (j ^ 1)
            step_swap.append((i * groups + j, target))
    pair = lax.ppermute(pair, "row", pair_swap)
    step = lax.ppermute(step, ("row", "ga"), step_swap)
    sums = conv(faces, table, places, folded)
    order = sorted(range(groups), key=lambda k: (offsets[k] > 0, offsets[k] < groups // 2, offsets[k]))
    root, empty, *sends = finish(places, sums, pair, step, root_bias, order, padded)
    come = sends[:1]
    for k, send in zip(order[1:], sends[1:]):
        come.append(lax.ppermute(send, "ga", [(i, i ^ offsets[k]) for i in range(groups)]))
    root_out, lift, weights, spread = unravel(
        root, w_down, w_skip, [offsets[k] for k in order], fine_feats.shape[2]
    )
    fine = fine_out(fine_feats, hidden, empty, lift, weights, spread, come)
    return (fine, root_out)


def solution(mesh):
    return jax.shard_map(
        shards,
        mesh=mesh,
        in_specs=(
            P(("row", "ga"), None, None),
            P(("row", "ga")),
            P(("row", "ga")),
            P(),
            P(),
            P("ga", None, None, None, None),
            P("ga"),
            P(),
            P(),
        ),
        out_specs=(P(("row", "ga"), None, None), P("ga", "row", None, None)),
        check_vma=False,
    )
```

```python
import functools

import jax
import jax.numpy as jnp
from jax import lax
from jax.experimental import pallas as pl
from jax.experimental.pallas import tpu as pltpu
from jax.sharding import PartitionSpec as P

B = 8
RXY = 32
RZ_REG = 4

HALF = B // 2
OCT = RXY // 2
LAYERS = RZ_REG // 2
PLANE = OCT * OCT
INNER = (1, 2)
OUTER = (0, 3)
BORDERED = PLANE + 2 * OCT
SUBS = 8
HALVES = SUBS // 2
META = 16
BF16 = jnp.bfloat16
F32 = jnp.float32
VMEM = pl.BlockSpec(memory_space=pltpu.VMEM)
ANY = pl.BlockSpec(memory_space=pl.ANY)


def params(mib):
    return pltpu.CompilerParams(vmem_limit_bytes=mib << 20)


def cost(macs, moved):
    return pl.CostEstimate(flops=2 * macs, bytes_accessed=moved, transcendentals=0)


def iota(shape, axis):
    return lax.broadcasted_iota(jnp.int32, shape, axis)


def dot(left, right):
    return jnp.dot(left, right, preferred_element_type=F32)


def dot_nt(left, right):
    return lax.dot_general(left, right, (((1,), (1,)), ((), ())), preferred_element_type=F32)


def hidden_voxel(fine):
    edge = B.bit_length() - 1
    z, y, x = fine >> 2 * edge, fine >> edge & B - 1, fine & B - 1
    low = (z >> 1 & 1) * 4 + (y >> 1 & 1) * 2 + (x >> 1 & 1)
    high = (z >> edge - 1) * 4 + (y >> edge - 1) * 2 + (x >> edge - 1)
    return low * SUBS + high


def run_bounds(count):
    cuts = [0]
    while cuts[-1] < count:
        cuts.append(min(2 * cuts[-1] + 1, count))
    return list(zip(cuts, cuts[1:]))


def repeat_blocks(ref, block):
    rows, columns = block.shape
    ref[...] = jnp.zeros_like(ref)
    for s in range(ref.shape[0] // rows):
        ref[s * rows : (s + 1) * rows, s * columns : (s + 1) * columns] = block


def parts_of(total, group, most):
    return max(n for n in range(group, most + 1, group) if total % n == 0)


def fine_in_kernel(
    child_hbm, block_hbm, fine_hbm, w_hbm, turned_hbm, pooled_ref, rest_ref,
    fine_ref, child_ref, block_ref, w_ref, pool, weights, turned, tops, meta, fine_sems, turned_sems, sems, *, total, padded
):
    _, width, voxels = fine_ref.shape
    depth = w_ref.shape[1]
    group = turned.shape[1] // width
    cells = voxels // SUBS
    chunk = total // fine_sems.shape[0]
    sets = chunk // group

    def fetch(i):
        part = pl.ds(i * chunk, chunk)
        return pltpu.make_async_copy(fine_hbm.at[part], fine_ref.at[part], fine_sems.at[i])

    def store(low, high):
        part = pl.ds(low * sets * cells, (high - low) * sets * cells)
        return pltpu.make_async_copy(turned.at[part], turned_hbm.at[part], turned_sems.at[low])

    fetch(0).start(priority=1)
    small = [
        pltpu.make_async_copy(source, target, sems.at[i])
        for i, (source, target) in enumerate(
            ((w_hbm, w_ref), (child_hbm, child_ref), (block_hbm, block_ref))
        )
    ]
    for copy in small:
        copy.start()
    for i in range(1, total // chunk):
        fetch(i).start(priority=1)

    hit = hidden_voxel(iota((voxels, cells), 0)) == iota((voxels, cells), 1)
    pool[...] = jnp.where(hit, 1.0 / SUBS, 0.0).astype(BF16)
    for copy in small:
        copy.wait()
    repeat_blocks(weights, w_ref[...])
    meta[...] = jnp.full_like(meta, -1.0)
    meta[0:1, 0:total] = (child_ref[...] >> 3).astype(F32)
    meta[1:2, 0:total] = (child_ref[...] & 7).astype(F32)
    meta[2:3, 0 : block_ref.shape[1]] = block_ref[...].astype(F32)
    pooled_ref[HALVES * padded : HALVES * padded + META, :] = meta[...].astype(BF16)

    def project(low, high):
        rows = turned[low * sets * cells : high * sets * cells, :]
        hidden = jnp.maximum(dot(rows, weights[...]), 0.0).astype(BF16)
        cubes = hidden.astype(F32).reshape((high - low) * sets, SUBS, SUBS, group * depth)
        top = jnp.sum(cubes, axis=1) * (1.0 / SUBS)
        for g in range((high - low) * sets):
            for s in range(group):
                at = (low * chunk + g * group + s) * SUBS
                tops[at : at + SUBS, :] = top[g, :, s * depth : (s + 1) * depth]

    runs = run_bounds(total // chunk)
    for low, high in runs:
        if low and high == total // chunk:
            project(0, low)
        for i in range(low, high):
            fetch(i).wait()
        cube = fine_ref[low * chunk : high * chunk].reshape((high - low) * chunk * width, voxels)
        octants = dot(cube, pool[...]).astype(BF16)
        for g in range((high - low) * sets):
            at = (low * sets + g) * cells
            turned[at : at + cells, :] = octants[g * group * width : (g + 1) * group * width].T
        store(low, high).start()
    project(*runs[-1])
    if padded != total:
        tops[total * SUBS :, :] = jnp.zeros(((padded - total) * SUBS, depth), F32)
    for v in range(SUBS):
        half_ref = pooled_ref if v < HALVES else rest_ref
        first = v % HALVES * padded
        half_ref[first : first + padded, :] = tops[pl.ds(v, padded, stride=SUBS), :].astype(BF16)
    for low, high in runs:
        store(low, high).wait()


def fine_in(fine_feats, fine_child, parent_block, w_parent, padded):
    total, width, voxels = fine_feats.shape
    depth = w_parent.shape[1]
    pairs = parent_block.shape[0]
    group = 256 // width
    cells = voxels // SUBS
    chunk = parts_of(total, group, 16)
    return pl.pallas_call(
        functools.partial(fine_in_kernel, total=total, padded=padded),
        in_specs=[ANY] * 4,
        out_specs=[ANY, VMEM, VMEM],
        out_shape=[
            jax.ShapeDtypeStruct((total // group * cells, group * width), BF16),
            jax.ShapeDtypeStruct((HALVES * padded + META, depth), BF16),
            jax.ShapeDtypeStruct((HALVES * padded, depth), BF16),
        ],
        scratch_shapes=[
            pltpu.VMEM(fine_feats.shape, BF16),
            pltpu.VMEM((1, total), jnp.int32),
            pltpu.VMEM((1, pairs), jnp.int32),
            pltpu.VMEM(w_parent.shape, BF16),
            pltpu.VMEM((voxels, cells), BF16),
            pltpu.VMEM((group * width, group * depth), BF16),
            pltpu.VMEM((total // group * cells, group * width), BF16),
            pltpu.VMEM((padded * SUBS, depth), F32),
            pltpu.VMEM((META, 128), F32),
            pltpu.SemaphoreType.DMA((total // chunk,)),
            pltpu.SemaphoreType.DMA((total // chunk,)),
            pltpu.SemaphoreType.DMA((3,)),
        ],
        compiler_params=params(58),
        cost_estimate=cost(total * width * voxels * 256, 2 * total * width * voxels),
        name="fine_in",
    )(fine_child[None], parent_block[None], fine_feats, w_parent)


def hide_kernel(turned_ref, w_ref, hidden_ref, weights):
    repeat_blocks(weights, w_ref[...])
    hidden_ref[...] = jnp.maximum(dot(turned_ref[...], weights[...]), 0.0).astype(BF16)


def hide(turned, w_parent):
    width, depth = w_parent.shape
    rows, wide = turned.shape
    return pl.pallas_call(
        hide_kernel,
        in_specs=[VMEM] * 2,
        out_specs=VMEM,
        out_shape=jax.ShapeDtypeStruct((rows, wide // width * depth), BF16),
        scratch_shapes=[pltpu.VMEM((wide, wide // width * depth), BF16)],
        compiler_params=params(12),
        cost_estimate=cost(rows * wide * 512, rows * wide * 6),
        name="hide",
    )(turned, w_parent)


def fold_kernel(w_ref, in_ref, out_ref):
    share = w_ref.shape[3]
    depth = in_ref.shape[0]
    nothing = jnp.zeros((share, w_ref.shape[4]), BF16)
    out_ref[:, 0, :, 2 * share :] = jnp.zeros((3, 4 * depth, 2 * share), BF16)
    out_ref[:, 3, :, 0 : 2 * share] = jnp.zeros((3, 4 * depth, 2 * share), BF16)
    for a in range(3):
        for b in range(3):
            for j in range(4):
                first = w_ref[a, b, j] if j < 3 else nothing
                second = w_ref[a, b, j - 1] if j > 0 else nothing
                pair = jnp.concatenate([first, second], axis=0)
                folded = dot_nt(in_ref[...], pair).astype(BF16)
                rows = slice(j * depth, (j + 1) * depth)
                out_ref[a, b, rows, 0 : 2 * share] = folded
                out_ref[a, b + 1, rows, 2 * share : 4 * share] = folded


def fold(w_root, w_root_in):
    share = w_root.shape[0]
    depth = w_root_in.shape[0]
    return pl.pallas_call(
        fold_kernel,
        in_specs=[VMEM, VMEM],
        out_specs=VMEM,
        out_shape=jax.ShapeDtypeStruct((3, 4, 4 * depth, 4 * share), BF16),
        compiler_params=params(16),
        cost_estimate=cost(36 * depth * 256 * 128, 6 << 20),
        name="fold",
    )(w_root.transpose(2, 3, 4, 0, 1), w_root_in)


def y_window(j):
    return ((1, 0), (0, OCT), (1, OCT), (0, 2 * OCT))[j]


def fill_planes(planes_ref, planes, place, table):
    depth = table.shape[1] // SUBS
    x = place % OCT
    planes_ref[:, :, 0:OCT, :] = jnp.zeros((2, LAYERS, OCT, 4 * depth), BF16)
    planes_ref[:, :, OCT + PLANE :, :] = jnp.zeros((2, LAYERS, OCT, 4 * depth), BF16)
    live = place >= 0
    shifted = (
        (0, 1, jnp.where(live & (x < OCT - 1), place + 1, -1)),
        (1, 0, place),
        (2, 1, place),
        (3, 0, jnp.where(live & (x > 0), place - 1, -1)),
    )
    for j, vx, at in shifted:
        hot = jnp.where(iota((LAYERS * PLANE, place.shape[1]), 0) == at, 1.0, 0.0).astype(BF16)
        for layer, z in enumerate(planes):
            first = (vx * 4 + z % 2 * 2) * depth
            both = dot(hot[layer * PLANE : (layer + 1) * PLANE], table[:, first : first + 2 * depth]).astype(BF16)
            for vy in range(2):
                planes_ref[vy, layer, OCT : OCT + PLANE, j * depth : (j + 1) * depth] = both[
                    :, vy * depth : (vy + 1) * depth
                ]


def place_kernel(offsets, padded, pairs, *refs):
    groups = len(offsets)
    pooled_refs, rest_refs, w_ref = refs[:groups], refs[groups : 2 * groups], refs[2 * groups]
    faces_ref, table, place_ref, pair_ref, step_ref = refs[2 * groups + 1 :]
    depth = pooled_refs[0].shape[1]
    lane_count = groups * 128
    me = lax.axis_index("ga")
    row = lax.axis_index("row")

    metas = [r[HALVES * padded : HALVES * padded + META, :] for r in pooled_refs]
    parent = jnp.concatenate([m[0:1].astype(F32) for m in metas], axis=1).astype(jnp.int32)
    octant = jnp.concatenate([m[1:2].astype(F32) for m in metas], axis=1).astype(jnp.int32)
    found = jnp.zeros((META, lane_count), F32)
    for k, offset in enumerate(offsets):
        at = iota((128, lane_count), 0)
        hot = (at < pairs) & (parent == at + (me ^ offset) * pairs)
        found += dot(metas[k], jnp.where(hot, 1.0, 0.0).astype(BF16))
    block = found[2:3].astype(jnp.int32)
    side = RXY // HALF
    z = block // (side * side) * 2 + (octant >> 2)
    y = block // side % side * 2 + (octant >> 1) % 2
    x = block % side * 2 + octant % 2
    live = parent >= 0
    place = jnp.where(live, (z * OCT + y) * OCT + x, -1)
    place_ref[...] = jnp.broadcast_to(place, place_ref.shape)

    for k in range(groups):
        for v in range(SUBS):
            half_ref, first = (pooled_refs, rest_refs)[v // HALVES][k], v % HALVES * padded
            vz, vy, vx = v >> 2, v >> 1 & 1, v & 1
            lanes = slice((vx * 4 + vz * 2 + vy) * depth, (vx * 4 + vz * 2 + vy + 1) * depth)
            table[k * 128 : k * 128 + padded, lanes] = half_ref[first : first + padded, :]
            if padded < 128:
                table[k * 128 + padded : (k + 1) * 128, lanes] = jnp.zeros((128 - padded, depth), BF16)

    fill_planes(faces_ref, OUTER, place, table)

    even = row % 2 == 0
    for out_ref, up in ((pair_ref, even), (step_ref, jnp.logical_not(even))):
        plane = jnp.where(up, 1, 0)
        dz = jnp.where(up, 0, 2)
        total = None
        for j in range(4):
            vy, first = y_window(j)
            part = dot(faces_ref[vy, plane, first : first + PLANE, :], w_ref[dz, j])
            total = part if total is None else total + part
        out_ref[...] = total.astype(BF16)


def place(pooled, rest, offsets, folded, padded, pairs):
    groups = len(offsets)
    depth = pooled[0].shape[1]
    wide = folded.shape[3]
    return pl.pallas_call(
        functools.partial(place_kernel, offsets, padded, pairs),
        in_specs=[VMEM] * (2 * groups + 1),
        out_specs=[VMEM] * 5,
        out_shape=[
            jax.ShapeDtypeStruct((2, LAYERS, BORDERED, 4 * depth), BF16),
            jax.ShapeDtypeStruct((groups * 128, SUBS * depth), BF16),
            jax.ShapeDtypeStruct((8, groups * 128), jnp.int32),
            jax.ShapeDtypeStruct((PLANE, wide), BF16),
            jax.ShapeDtypeStruct((PLANE, wide), BF16),
        ],
        compiler_params=params(16),
        cost_estimate=cost(1 << 28, 6 << 20),
        name="place",
    )(*pooled, *rest, folded)


def conv_kernel(faces_ref, table_ref, place_ref, w_ref, out_ref, inside):
    fill_planes(inside, INNER, place_ref[0:1, :], table_ref)
    for z in range(RZ_REG):
        total = None
        for a in range(3):
            source = z + a - 1
            if not 0 <= source < RZ_REG:
                continue
            planes = inside if source in INNER else faces_ref
            for j in range(4):
                vy, first = y_window(j)
                part = dot(planes[vy, source // 2, first : first + PLANE, :], w_ref[a, j])
                total = part if total is None else total + part
        out_ref[z] = total


def conv(faces, table, places, folded):
    wide = folded.shape[3]
    return pl.pallas_call(
        conv_kernel,
        in_specs=[VMEM] * 4,
        out_specs=VMEM,
        out_shape=jax.ShapeDtypeStruct((RZ_REG, PLANE, wide), F32),
        scratch_shapes=[pltpu.VMEM(faces.shape, BF16)],
        compiler_params=params(20),
        cost_estimate=cost(10 * 4 * PLANE * 512 * 256, 6 << 20),
        name="conv",
    )(faces, table, places, folded)


def finish_kernel(padded, order, place_ref, sums_ref, pair_ref, step_ref, bias_ref, *refs):
    root_ref, empty_ref, send_refs = refs[0], refs[1], refs[2:]
    lane_count = place_ref.shape[1]
    row = lax.axis_index("row")
    even = row % 2 == 0
    last = lax.axis_size("row") - 1
    bias = jnp.concatenate([bias_ref[...]] * 4, axis=1)
    pair = pair_ref[...].astype(F32)
    step = step_ref[...].astype(F32)
    above = jnp.where(even, pair, step)
    below = jnp.where(even, step, pair)
    above = jnp.where(row < last, above, 0.0)
    below = jnp.where(row > 0, below, 0.0)
    column = place_ref[...].astype(F32).T[:, 0:1].astype(jnp.int32)
    empty_ref[...] = jnp.broadcast_to(jnp.where(column[0:padded] < 0, -1e30, 0.0), empty_ref.shape)
    hot = jnp.where(column == iota((lane_count, LAYERS * PLANE), 1), 1.0, 0.0).astype(BF16)
    for z in range(RZ_REG):
        total = sums_ref[z] + bias
        if z == 0:
            total += below
        if z == RZ_REG - 1:
            total += above
        root_ref[z % 2, z // 2 * PLANE : (z // 2 + 1) * PLANE, :] = jnp.maximum(total, 0.0).astype(BF16)
    wide = root_ref.shape[2]
    for vz in range(2):
        picked = dot(hot, root_ref[vz]).astype(BF16)
        for send_ref, k in zip(send_refs, order):
            send_ref[:, vz * wide : (vz + 1) * wide] = picked[k * 128 : k * 128 + padded]


def finish(places, sums, pair, step, root_bias, order, padded):
    wide = sums.shape[2]
    groups = len(order)
    return pl.pallas_call(
        functools.partial(finish_kernel, padded, order),
        in_specs=[VMEM] * 5,
        out_specs=[VMEM] * (groups + 2),
        out_shape=[
            jax.ShapeDtypeStruct((2, LAYERS * PLANE, wide), BF16),
            jax.ShapeDtypeStruct((padded, 128), F32),
        ]
        + [jax.ShapeDtypeStruct((padded, 2 * wide), BF16)] * groups,
        compiler_params=params(24),
        cost_estimate=cost(1 << 27, 3 << 20),
        name="finish",
    )(places, sums, pair, step, root_bias[None])


def unravel_kernel(offsets, root_ref, down_ref, skip_ref, out_ref, lift_ref, weights_ref, spread_ref):
    share = root_ref.shape[2] // 4
    rows, half = PLANE, PLANE // 2
    x, y = iota((rows, half), 0), iota((rows, half), 1)
    same = x // RXY == y // OCT
    spread = [
        jnp.where(same & (x % RXY == 2 * (y % OCT) + vx), 1.0, 0.0).astype(BF16) for vx in range(2)
    ]
    lines = half // OCT
    for z in range(RZ_REG):
        for part in range(2):
            first = z // 2 * PLANE + part * half
            for vy in range(2):
                at = vy * 2 * share
                even = root_ref[z % 2, first : first + half, at : at + share]
                odd = root_ref[z % 2, first : first + half, at + share : at + 2 * share]
                line = (dot(spread[0], even) + dot(spread[1], odd)).astype(BF16)
                out_ref[z, part * lines : (part + 1) * lines, vy] = line.reshape(lines, RXY, share)

    me = lax.axis_index("ga")
    width, depth = skip_ref.shape
    lift_ref[...] = jnp.zeros_like(lift_ref)
    for k, offset in enumerate(offsets):
        own = down_ref[pl.ds(pl.multiple_of((me ^ offset) * share, share), share), :]
        for vx in range(2):
            first = (k * 2 + vx) * share
            lift_ref[first : first + share, vx * depth : (vx + 1) * depth] = own
    repeat_blocks(weights_ref, skip_ref[...].T)
    hit = hidden_voxel(iota(spread_ref.shape, 1)) == iota(spread_ref.shape, 0)
    spread_ref[...] = jnp.where(hit, 1.0, 0.0).astype(BF16)


def unravel(root, w_down, w_skip, offsets, voxels):
    share = root.shape[2] // 4
    depth, width = w_skip.shape
    group = 256 // width
    out, lift, weights, spread = pl.pallas_call(
        functools.partial(unravel_kernel, offsets),
        in_specs=[VMEM] * 3,
        out_specs=[VMEM] * 4,
        out_shape=[
            jax.ShapeDtypeStruct((RZ_REG, OCT, 2, RXY, share), BF16),
            jax.ShapeDtypeStruct((len(offsets) * 2 * share, 2 * depth), BF16),
            jax.ShapeDtypeStruct((group * depth, group * width), BF16),
            jax.ShapeDtypeStruct((voxels // SUBS, voxels), BF16),
        ],
        compiler_params=params(12),
        cost_estimate=cost(1 << 28, 2 << 20),
        name="unravel",
    )(root, w_down, w_skip.T)
    return out.reshape(RZ_REG, RXY, RXY, share).transpose(3, 0, 1, 2), lift, weights, spread


def fine_out_kernel(groups, *refs):
    fine_ref, hidden_ref, empty_ref, lift_ref, weights_ref, spread_ref = refs[:6]
    come_refs = refs[6 : 6 + groups]
    out_hbm, out_ref, lifted, skips, sems = refs[6 + groups :]
    total, width, voxels = fine_ref.shape
    depth = lift_ref.shape[1] // 2
    group = hidden_ref.shape[1] // depth
    cells = voxels // SUBS
    share = come_refs[0].shape[1] // SUBS
    chunk = total // sems.shape[0]
    sets = chunk // group

    for zy in range(4):
        lanes = slice(zy * 2 * share, (zy + 1) * 2 * share)
        both = dot(jnp.concatenate([r[:, lanes] for r in come_refs], axis=1), lift_ref[...])
        slots = both.shape[0]
        for vx in range(2):
            top = both[:, vx * depth : (vx + 1) * depth] + empty_ref[...]
            lifted[pl.ds(zy * 2 + vx, slots, stride=SUBS), :] = top

    for i in range(total // chunk):
        rows = []
        for g in range(sets):
            at = i * sets + g
            tops = [
                lifted[(at * group + s) * SUBS : (at * group + s + 1) * SUBS, :] for s in range(group)
            ]
            hidden = hidden_ref[at * cells : (at + 1) * cells, :].astype(F32).reshape(SUBS, SUBS, group * depth)
            decoded = jnp.maximum(hidden + jnp.concatenate(tops, axis=1)[None], 0.0)
            rows.append(decoded.reshape(cells, group * depth).astype(BF16))
        skip = dot(jnp.concatenate(rows, axis=0), weights_ref[...]).astype(BF16)
        for g in range(sets):
            at = (i * sets + g) * group * width
            skips[at : at + group * width, :] = skip[g * cells : (g + 1) * cells].T

    def send(i):
        part = pl.ds(i * chunk, chunk)
        return pltpu.make_async_copy(out_ref.at[part], out_hbm.at[part], sems.at[i])

    for i in range(total // chunk):
        part = slice(i * chunk, (i + 1) * chunk)
        up = dot(skips[i * chunk * width : (i + 1) * chunk * width, :], spread_ref[...])
        cube = fine_ref[part].reshape(chunk * width, voxels)
        out_ref[part] = (cube.astype(F32) + up).astype(BF16).reshape(chunk, width, voxels)
        send(i).start()
    for i in range(total // chunk):
        send(i).wait()


def fine_out(fine_feats, hidden, empty, lift, weights, spread, come):
    total, width, voxels = fine_feats.shape
    padded = empty.shape[0]
    depth = lift.shape[1] // 2
    group = 256 // width
    groups = len(come)
    chunk = parts_of(total, group, 16)
    return pl.pallas_call(
        functools.partial(fine_out_kernel, groups),
        in_specs=[VMEM] * (6 + groups),
        out_specs=ANY,
        out_shape=jax.ShapeDtypeStruct(fine_feats.shape, BF16),
        scratch_shapes=[
            pltpu.VMEM(fine_feats.shape, BF16),
            pltpu.VMEM((padded * SUBS, depth), F32),
            pltpu.VMEM((total * width, voxels // SUBS), BF16),
            pltpu.SemaphoreType.DMA((total // chunk,)),
        ],
        compiler_params=params(28),
        cost_estimate=cost(total * width * voxels * 256, 4 * total * width * voxels),
        name="fine_out",
    )(fine_feats, hidden, empty, lift, weights, spread, *come)


def shards(
    fine_feats, fine_child, parent_block, w_parent, w_root_in, w_root, root_bias, w_down, w_skip
):
    groups = lax.axis_size("ga")
    rows = lax.axis_size("row")
    slots = fine_feats.shape[0]
    padded = -(-slots // META) * META
    pairs = parent_block.shape[0]

    turned, pooled, rest = fine_in(fine_feats, fine_child, parent_block, w_parent, padded)

    hidden = hide(turned, w_parent)
    folded = fold(w_root, w_root_in)

    gathered, others, offsets = [pooled], [rest], [0]
    bit = groups // 2
    while bit:
        swap = [(i, i ^ bit) for i in range(groups)]
        gathered += [lax.ppermute(part, "ga", swap) for part in gathered]
        others += [lax.ppermute(part, "ga", swap) for part in others]
        offsets += [offset ^ bit for offset in offsets]
        if bit == groups // 2:
            others[1], folded, hidden = lax.optimization_barrier((others[1], folded, hidden))
        bit //= 2
    offsets = tuple(offsets)

    faces, table, places, pair, step = place(gathered, others, offsets, folded, padded, pairs)
    pair_swap = [(i, i ^ 1) for i in range(rows) if i ^ 1 < rows]
    step_swap = []
    for i in range(rows):
        inner = 0 < i < rows - 1
        for j in range(groups):
            target = ((i - 1 ^ 1) + 1) * groups + j if inner else i * groups + (j ^ 1)
            step_swap.append((i * groups + j, target))
    pair = lax.ppermute(pair, "row", pair_swap)
    step = lax.ppermute(step, ("row", "ga"), step_swap)
    sums = conv(faces, table, places, folded)
    order = sorted(range(groups), key=lambda k: (offsets[k] > 0, offsets[k] < groups // 2, offsets[k]))
    root, empty, *sends = finish(places, sums, pair, step, root_bias, order, padded)
    come = sends[:1]
    for k, send in zip(order[1:], sends[1:]):
        come.append(lax.ppermute(send, "ga", [(i, i ^ offsets[k]) for i in range(groups)]))
    root_out, lift, weights, spread = unravel(
        root, w_down, w_skip, [offsets[k] for k in order], fine_feats.shape[2]
    )
    fine = fine_out(fine_feats, hidden, empty, lift, weights, spread, come)
    return (fine, root_out)


def solution(mesh):
    return jax.shard_map(
        shards,
        mesh=mesh,
        in_specs=(
            P(("row", "ga"), None, None),
            P(("row", "ga")),
            P(("row", "ga")),
            P(),
            P(),
            P("ga", None, None, None, None),
            P("ga"),
            P(),
            P(),
        ),
        out_specs=(P(("row", "ga"), None, None), P("ga", "row", None, None)),
        check_vma=False,
    )
```

```python
import functools

import jax
import jax.numpy as jnp
from jax import lax
from jax.experimental import pallas as pl
from jax.experimental.pallas import tpu as pltpu
from jax.sharding import PartitionSpec as P

B = 8
RXY = 32
RZ_REG = 4

HALF = B // 2
OCT = RXY // 2
LAYERS = RZ_REG // 2
PLANE = OCT * OCT
INNER = (1, 2)
OUTER = (0, 3)
BORDERED = PLANE + 2 * OCT
SUBS = 8
HALVES = SUBS // 2
META = 16
BF16 = jnp.bfloat16
F32 = jnp.float32
VMEM = pl.BlockSpec(memory_space=pltpu.VMEM)
ANY = pl.BlockSpec(memory_space=pl.ANY)


def params(mib):
    return pltpu.CompilerParams(vmem_limit_bytes=mib << 20)


def cost(macs, moved):
    return pl.CostEstimate(flops=2 * macs, bytes_accessed=moved, transcendentals=0)


def iota(shape, axis):
    return lax.broadcasted_iota(jnp.int32, shape, axis)


def dot(left, right):
    return jnp.dot(left, right, preferred_element_type=F32)


def dot_nt(left, right):
    return lax.dot_general(left, right, (((1,), (1,)), ((), ())), preferred_element_type=F32)


def hidden_voxel(fine):
    edge = B.bit_length() - 1
    z, y, x = fine >> 2 * edge, fine >> edge & B - 1, fine & B - 1
    low = (z >> 1 & 1) * 4 + (y >> 1 & 1) * 2 + (x >> 1 & 1)
    high = (z >> edge - 1) * 4 + (y >> edge - 1) * 2 + (x >> edge - 1)
    return low * SUBS + high


def run_bounds(count):
    cuts = [0]
    while cuts[-1] < count:
        cuts.append(min(2 * cuts[-1] + 1, count))
    return list(zip(cuts, cuts[1:]))


def repeat_blocks(ref, block):
    rows, columns = block.shape
    ref[...] = jnp.zeros_like(ref)
    for s in range(ref.shape[0] // rows):
        ref[s * rows : (s + 1) * rows, s * columns : (s + 1) * columns] = block


def parts_of(total, group, most):
    return max(n for n in range(group, most + 1, group) if total % n == 0)


def fine_in_kernel(
    child_hbm, block_hbm, fine_hbm, w_hbm, turned_hbm, pooled_ref, rest_ref,
    fine_ref, child_ref, block_ref, w_ref, pool, weights, turned, tops, meta, fine_sems, turned_sems, sems, *, total, padded
):
    _, width, voxels = fine_ref.shape
    depth = w_ref.shape[1]
    group = turned.shape[1] // width
    cells = voxels // SUBS
    chunk = total // fine_sems.shape[0]
    sets = chunk // group

    def fetch(i):
        part = pl.ds(i * chunk, chunk)
        return pltpu.make_async_copy(fine_hbm.at[part], fine_ref.at[part], fine_sems.at[i])

    def store(low, high):
        part = pl.ds(low * sets * cells, (high - low) * sets * cells)
        return pltpu.make_async_copy(turned.at[part], turned_hbm.at[part], turned_sems.at[low])

    fetch(0).start(priority=1)
    small = [
        pltpu.make_async_copy(source, target, sems.at[i])
        for i, (source, target) in enumerate(
            ((w_hbm, w_ref), (child_hbm, child_ref), (block_hbm, block_ref))
        )
    ]
    for copy in small:
        copy.start()
    for i in range(1, total // chunk):
        fetch(i).start(priority=1)

    hit = hidden_voxel(iota((voxels, cells), 0)) == iota((voxels, cells), 1)
    pool[...] = jnp.where(hit, 1.0 / SUBS, 0.0).astype(BF16)
    for copy in small:
        copy.wait()
    repeat_blocks(weights, w_ref[...])
    meta[...] = jnp.full_like(meta, -1.0)
    meta[0:1, 0:total] = (child_ref[...] >> 3).astype(F32)
    meta[1:2, 0:total] = (child_ref[...] & 7).astype(F32)
    meta[2:3, 0 : block_ref.shape[1]] = block_ref[...].astype(F32)
    pooled_ref[HALVES * padded : HALVES * padded + META, :] = meta[...].astype(BF16)

    def project(low, high):
        rows = turned[low * sets * cells : high * sets * cells, :]
        hidden = jnp.maximum(dot(rows, weights[...]), 0.0).astype(BF16)
        cubes = hidden.astype(F32).reshape((high - low) * sets, SUBS, SUBS, group * depth)
        top = jnp.sum(cubes, axis=1) * (1.0 / SUBS)
        for g in range((high - low) * sets):
            for s in range(group):
                at = (low * chunk + g * group + s) * SUBS
                tops[at : at + SUBS, :] = top[g, :, s * depth : (s + 1) * depth]

    runs = run_bounds(total // chunk)
    for low, high in runs:
        if low and high == total // chunk:
            project(0, low)
        for i in range(low, high):
            fetch(i).wait()
        cube = fine_ref[low * chunk : high * chunk].reshape((high - low) * chunk * width, voxels)
        octants = dot(cube, pool[...]).astype(BF16)
        for g in range((high - low) * sets):
            at = (low * sets + g) * cells
            turned[at : at + cells, :] = octants[g * group * width : (g + 1) * group * width].T
        store(low, high).start()
    project(*runs[-1])
    if padded != total:
        tops[total * SUBS :, :] = jnp.zeros(((padded - total) * SUBS, depth), F32)
    for v in range(SUBS):
        half_ref = pooled_ref if v < HALVES else rest_ref
        first = v % HALVES * padded
        half_ref[first : first + padded, :] = tops[pl.ds(v, padded, stride=SUBS), :].astype(BF16)
    for low, high in runs:
        store(low, high).wait()


def fine_in(fine_feats, fine_child, parent_block, w_parent, padded):
    total, width, voxels = fine_feats.shape
    depth = w_parent.shape[1]
    pairs = parent_block.shape[0]
    group = 256 // width
    cells = voxels // SUBS
    chunk = parts_of(total, group, 16)
    return pl.pallas_call(
        functools.partial(fine_in_kernel, total=total, padded=padded),
        in_specs=[ANY] * 4,
        out_specs=[ANY, VMEM, VMEM],
        out_shape=[
            jax.ShapeDtypeStruct((total // group * cells, group * width), BF16),
            jax.ShapeDtypeStruct((HALVES * padded + META, depth), BF16),
            jax.ShapeDtypeStruct((HALVES * padded, depth), BF16),
        ],
        scratch_shapes=[
            pltpu.VMEM(fine_feats.shape, BF16),
            pltpu.VMEM((1, total), jnp.int32),
            pltpu.VMEM((1, pairs), jnp.int32),
            pltpu.VMEM(w_parent.shape, BF16),
            pltpu.VMEM((voxels, cells), BF16),
            pltpu.VMEM((group * width, group * depth), BF16),
            pltpu.VMEM((total // group * cells, group * width), BF16),
            pltpu.VMEM((padded * SUBS, depth), F32),
            pltpu.VMEM((META, 128), F32),
            pltpu.SemaphoreType.DMA((total // chunk,)),
            pltpu.SemaphoreType.DMA((total // chunk,)),
            pltpu.SemaphoreType.DMA((3,)),
        ],
        compiler_params=params(58),
        cost_estimate=cost(total * width * voxels * 256, 2 * total * width * voxels),
        name="fine_in",
    )(fine_child[None], parent_block[None], fine_feats, w_parent)


def hide_kernel(turned_ref, w_ref, hidden_ref, weights):
    repeat_blocks(weights, w_ref[...])
    hidden_ref[...] = jnp.maximum(dot(turned_ref[...], weights[...]), 0.0).astype(BF16)


def hide(turned, w_parent):
    width, depth = w_parent.shape
    rows, wide = turned.shape
    return pl.pallas_call(
        hide_kernel,
        in_specs=[VMEM] * 2,
        out_specs=VMEM,
        out_shape=jax.ShapeDtypeStruct((rows, wide // width * depth), BF16),
        scratch_shapes=[pltpu.VMEM((wide, wide // width * depth), BF16)],
        compiler_params=params(12),
        cost_estimate=cost(rows * wide * 512, rows * wide * 6),
        name="hide",
    )(turned, w_parent)


def fold_kernel(w_ref, in_ref, out_ref):
    share = w_ref.shape[3]
    depth = in_ref.shape[0]
    nothing = jnp.zeros((share, w_ref.shape[4]), BF16)
    out_ref[:, 0, :, 2 * share :] = jnp.zeros((3, 4 * depth, 2 * share), BF16)
    out_ref[:, 3, :, 0 : 2 * share] = jnp.zeros((3, 4 * depth, 2 * share), BF16)
    for a in range(3):
        for b in range(3):
            for j in range(4):
                first = w_ref[a, b, j] if j < 3 else nothing
                second = w_ref[a, b, j - 1] if j > 0 else nothing
                pair = jnp.concatenate([first, second], axis=0)
                folded = dot_nt(in_ref[...], pair).astype(BF16)
                rows = slice(j * depth, (j + 1) * depth)
                out_ref[a, b, rows, 0 : 2 * share] = folded
                out_ref[a, b + 1, rows, 2 * share : 4 * share] = folded


def fold(w_root, w_root_in):
    share = w_root.shape[0]
    depth = w_root_in.shape[0]
    return pl.pallas_call(
        fold_kernel,
        in_specs=[VMEM, VMEM],
        out_specs=VMEM,
        out_shape=jax.ShapeDtypeStruct((3, 4, 4 * depth, 4 * share), BF16),
        compiler_params=params(16),
        cost_estimate=cost(36 * depth * 256 * 128, 6 << 20),
        name="fold",
    )(w_root.transpose(2, 3, 4, 0, 1), w_root_in)


def y_window(j):
    return ((1, 0), (0, OCT), (1, OCT), (0, 2 * OCT))[j]


def fill_planes(planes_ref, planes, place, table):
    depth = table.shape[1] // SUBS
    x = place % OCT
    planes_ref[:, :, 0:OCT, :] = jnp.zeros((2, LAYERS, OCT, 4 * depth), BF16)
    planes_ref[:, :, OCT + PLANE :, :] = jnp.zeros((2, LAYERS, OCT, 4 * depth), BF16)
    live = place >= 0
    shifted = (
        (0, 1, jnp.where(live & (x < OCT - 1), place + 1, -1)),
        (1, 0, place),
        (2, 1, place),
        (3, 0, jnp.where(live & (x > 0), place - 1, -1)),
    )
    for j, vx, at in shifted:
        hot = jnp.where(iota((LAYERS * PLANE, place.shape[1]), 0) == at, 1.0, 0.0).astype(BF16)
        for layer, z in enumerate(planes):
            first = (vx * 4 + z % 2 * 2) * depth
            both = dot(hot[layer * PLANE : (layer + 1) * PLANE], table[:, first : first + 2 * depth]).astype(BF16)
            for vy in range(2):
                planes_ref[vy, layer, OCT : OCT + PLANE, j * depth : (j + 1) * depth] = both[
                    :, vy * depth : (vy + 1) * depth
                ]


def place_kernel(offsets, padded, pairs, *refs):
    groups = len(offsets)
    pooled_refs, rest_refs, w_ref = refs[:groups], refs[groups : 2 * groups], refs[2 * groups]
    faces_ref, table, place_ref, pair_ref, step_ref = refs[2 * groups + 1 :]
    depth = pooled_refs[0].shape[1]
    lane_count = groups * 128
    me = lax.axis_index("ga")
    row = lax.axis_index("row")

    metas = [r[HALVES * padded : HALVES * padded + META, :] for r in pooled_refs]
    parent = jnp.concatenate([m[0:1].astype(F32) for m in metas], axis=1).astype(jnp.int32)
    octant = jnp.concatenate([m[1:2].astype(F32) for m in metas], axis=1).astype(jnp.int32)
    found = jnp.zeros((META, lane_count), F32)
    for k, offset in enumerate(offsets):
        at = iota((128, lane_count), 0)
        hot = (at < pairs) & (parent == at + (me ^ offset) * pairs)
        found += dot(metas[k], jnp.where(hot, 1.0, 0.0).astype(BF16))
    block = found[2:3].astype(jnp.int32)
    side = RXY // HALF
    z = block // (side * side) * 2 + (octant >> 2)
    y = block // side % side * 2 + (octant >> 1) % 2
    x = block % side * 2 + octant % 2
    live = parent >= 0
    place = jnp.where(live, (z * OCT + y) * OCT + x, -1)
    place_ref[...] = jnp.broadcast_to(place, place_ref.shape)

    for k in range(groups):
        for v in range(SUBS):
            half_ref, first = (pooled_refs, rest_refs)[v // HALVES][k], v % HALVES * padded
            vz, vy, vx = v >> 2, v >> 1 & 1, v & 1
            lanes = slice((vx * 4 + vz * 2 + vy) * depth, (vx * 4 + vz * 2 + vy + 1) * depth)
            table[k * 128 : k * 128 + padded, lanes] = half_ref[first : first + padded, :]
            if padded < 128:
                table[k * 128 + padded : (k + 1) * 128, lanes] = jnp.zeros((128 - padded, depth), BF16)

    fill_planes(faces_ref, OUTER, place, table)

    even = row % 2 == 0
    for out_ref, up in ((pair_ref, even), (step_ref, jnp.logical_not(even))):
        plane = jnp.where(up, 1, 0)
        dz = jnp.where(up, 0, 2)
        total = None
        for j in range(4):
            vy, first = y_window(j)
            part = dot(faces_ref[vy, plane, first : first + PLANE, :], w_ref[dz, j])
            total = part if total is None else total + part
        out_ref[...] = total.astype(BF16)


def place(pooled, rest, offsets, folded, padded, pairs):
    groups = len(offsets)
    depth = pooled[0].shape[1]
    wide = folded.shape[3]
    return pl.pallas_call(
        functools.partial(place_kernel, offsets, padded, pairs),
        in_specs=[VMEM] * (2 * groups + 1),
        out_specs=[VMEM] * 5,
        out_shape=[
            jax.ShapeDtypeStruct((2, LAYERS, BORDERED, 4 * depth), BF16),
            jax.ShapeDtypeStruct((groups * 128, SUBS * depth), BF16),
            jax.ShapeDtypeStruct((8, groups * 128), jnp.int32),
            jax.ShapeDtypeStruct((PLANE, wide), BF16),
            jax.ShapeDtypeStruct((PLANE, wide), BF16),
        ],
        compiler_params=params(16),
        cost_estimate=cost(1 << 28, 6 << 20),
        name="place",
    )(*pooled, *rest, folded)


def conv_kernel(faces_ref, table_ref, place_ref, w_ref, out_ref, inside):
    fill_planes(inside, INNER, place_ref[0:1, :], table_ref)
    for z in range(RZ_REG):
        total = None
        for a in range(3):
            source = z + a - 1
            if not 0 <= source < RZ_REG:
                continue
            planes = inside if source in INNER else faces_ref
            for j in range(4):
                vy, first = y_window(j)
                part = dot(planes[vy, source // 2, first : first + PLANE, :], w_ref[a, j])
                total = part if total is None else total + part
        out_ref[z] = total


def conv(faces, table, places, folded):
    wide = folded.shape[3]
    return pl.pallas_call(
        conv_kernel,
        in_specs=[VMEM] * 4,
        out_specs=VMEM,
        out_shape=jax.ShapeDtypeStruct((RZ_REG, PLANE, wide), F32),
        scratch_shapes=[pltpu.VMEM(faces.shape, BF16)],
        compiler_params=params(20),
        cost_estimate=cost(10 * 4 * PLANE * 512 * 256, 6 << 20),
        name="conv",
    )(faces, table, places, folded)


def finish_kernel(padded, order, place_ref, sums_ref, pair_ref, step_ref, bias_ref, *refs):
    root_ref, empty_ref, send_refs = refs[0], refs[1], refs[2:]
    lane_count = place_ref.shape[1]
    row = lax.axis_index("row")
    even = row % 2 == 0
    last = lax.axis_size("row") - 1
    bias = jnp.concatenate([bias_ref[...]] * 4, axis=1)
    pair = pair_ref[...].astype(F32)
    step = step_ref[...].astype(F32)
    above = jnp.where(even, pair, step)
    below = jnp.where(even, step, pair)
    above = jnp.where(row < last, above, 0.0)
    below = jnp.where(row > 0, below, 0.0)
    column = place_ref[...].astype(F32).T[:, 0:1].astype(jnp.int32)
    empty_ref[...] = jnp.broadcast_to(jnp.where(column[0:padded] < 0, -1e30, 0.0), empty_ref.shape)
    hot = jnp.where(column == iota((lane_count, LAYERS * PLANE), 1), 1.0, 0.0).astype(BF16)
    for z in range(RZ_REG):
        total = sums_ref[z] + bias
        if z == 0:
            total += below
        if z == RZ_REG - 1:
            total += above
        root_ref[z % 2, z // 2 * PLANE : (z // 2 + 1) * PLANE, :] = jnp.maximum(total, 0.0).astype(BF16)
    wide = root_ref.shape[2]
    for vz in range(2):
        picked = dot(hot, root_ref[vz]).astype(BF16)
        for send_ref, k in zip(send_refs, order):
            send_ref[:, vz * wide : (vz + 1) * wide] = picked[k * 128 : k * 128 + padded]


def finish(places, sums, pair, step, root_bias, order, padded):
    wide = sums.shape[2]
    groups = len(order)
    return pl.pallas_call(
        functools.partial(finish_kernel, padded, order),
        in_specs=[VMEM] * 5,
        out_specs=[VMEM] * (groups + 2),
        out_shape=[
            jax.ShapeDtypeStruct((2, LAYERS * PLANE, wide), BF16),
            jax.ShapeDtypeStruct((padded, 128), F32),
        ]
        + [jax.ShapeDtypeStruct((padded, 2 * wide), BF16)] * groups,
        compiler_params=params(24),
        cost_estimate=cost(1 << 27, 3 << 20),
        name="finish",
    )(places, sums, pair, step, root_bias[None])


def unravel_kernel(offsets, root_ref, down_ref, skip_ref, out_ref, lift_ref, weights_ref, spread_ref):
    share = root_ref.shape[2] // 4
    rows, half = PLANE, PLANE // 2
    x, y = iota((rows, half), 0), iota((rows, half), 1)
    same = x // RXY == y // OCT
    spread = [
        jnp.where(same & (x % RXY == 2 * (y % OCT) + vx), 1.0, 0.0).astype(BF16) for vx in range(2)
    ]
    lines = half // OCT
    for z in range(RZ_REG):
        for part in range(2):
            first = z // 2 * PLANE + part * half
            for vy in range(2):
                at = vy * 2 * share
                even = root_ref[z % 2, first : first + half, at : at + share]
                odd = root_ref[z % 2, first : first + half, at + share : at + 2 * share]
                line = (dot(spread[0], even) + dot(spread[1], odd)).astype(BF16)
                out_ref[z, part * lines : (part + 1) * lines, vy] = line.reshape(lines, RXY, share)

    me = lax.axis_index("ga")
    width, depth = skip_ref.shape
    lift_ref[...] = jnp.zeros_like(lift_ref)
    for k, offset in enumerate(offsets):
        own = down_ref[pl.ds(pl.multiple_of((me ^ offset) * share, share), share), :]
        for vx in range(2):
            first = (k * 2 + vx) * share
            lift_ref[first : first + share, vx * depth : (vx + 1) * depth] = own
    repeat_blocks(weights_ref, skip_ref[...].T)
    hit = hidden_voxel(iota(spread_ref.shape, 1)) == iota(spread_ref.shape, 0)
    spread_ref[...] = jnp.where(hit, 1.0, 0.0).astype(BF16)


def unravel(root, w_down, w_skip, offsets, voxels):
    share = root.shape[2] // 4
    depth, width = w_skip.shape
    group = 256 // width
    out, lift, weights, spread = pl.pallas_call(
        functools.partial(unravel_kernel, offsets),
        in_specs=[VMEM] * 3,
        out_specs=[VMEM] * 4,
        out_shape=[
            jax.ShapeDtypeStruct((RZ_REG, OCT, 2, RXY, share), BF16),
            jax.ShapeDtypeStruct((len(offsets) * 2 * share, 2 * depth), BF16),
            jax.ShapeDtypeStruct((group * depth, group * width), BF16),
            jax.ShapeDtypeStruct((voxels // SUBS, voxels), BF16),
        ],
        compiler_params=params(12),
        cost_estimate=cost(1 << 28, 2 << 20),
        name="unravel",
    )(root, w_down, w_skip.T)
    return out.reshape(RZ_REG, RXY, RXY, share).transpose(3, 0, 1, 2), lift, weights, spread


def fine_out_kernel(groups, *refs):
    fine_ref, hidden_ref, empty_ref, lift_ref, weights_ref, spread_ref = refs[:6]
    come_refs = refs[6 : 6 + groups]
    out_hbm, out_ref, lifted, skips, sems = refs[6 + groups :]
    total, width, voxels = fine_ref.shape
    depth = lift_ref.shape[1] // 2
    group = hidden_ref.shape[1] // depth
    cells = voxels // SUBS
    share = come_refs[0].shape[1] // SUBS
    chunk = total // sems.shape[0]
    sets = chunk // group

    for zy in range(4):
        lanes = slice(zy * 2 * share, (zy + 1) * 2 * share)
        both = dot(jnp.concatenate([r[:, lanes] for r in come_refs], axis=1), lift_ref[...])
        slots = both.shape[0]
        for vx in range(2):
            top = both[:, vx * depth : (vx + 1) * depth] + empty_ref[...]
            lifted[pl.ds(zy * 2 + vx, slots, stride=SUBS), :] = top

    for i in range(total // chunk):
        rows = []
        for g in range(sets):
            at = i * sets + g
            tops = [
                lifted[(at * group + s) * SUBS : (at * group + s + 1) * SUBS, :] for s in range(group)
            ]
            hidden = hidden_ref[at * cells : (at + 1) * cells, :].astype(F32).reshape(SUBS, SUBS, group * depth)
            decoded = jnp.maximum(hidden + jnp.concatenate(tops, axis=1)[None], 0.0)
            rows.append(decoded.reshape(cells, group * depth).astype(BF16))
        skip = dot(jnp.concatenate(rows, axis=0), weights_ref[...]).astype(BF16)
        for g in range(sets):
            at = (i * sets + g) * group * width
            skips[at : at + group * width, :] = skip[g * cells : (g + 1) * cells].T

    def send(i):
        part = pl.ds(i * chunk, chunk)
        return pltpu.make_async_copy(out_ref.at[part], out_hbm.at[part], sems.at[i])

    for i in range(total // chunk):
        part = slice(i * chunk, (i + 1) * chunk)
        up = dot(skips[i * chunk * width : (i + 1) * chunk * width, :], spread_ref[...])
        cube = fine_ref[part].reshape(chunk * width, voxels)
        out_ref[part] = (cube.astype(F32) + up).astype(BF16).reshape(chunk, width, voxels)
        send(i).start()
    for i in range(total // chunk):
        send(i).wait()


def fine_out(fine_feats, hidden, empty, lift, weights, spread, come):
    total, width, voxels = fine_feats.shape
    padded = empty.shape[0]
    depth = lift.shape[1] // 2
    group = 256 // width
    groups = len(come)
    chunk = parts_of(total, group, 8)
    return pl.pallas_call(
        functools.partial(fine_out_kernel, groups),
        in_specs=[VMEM] * (6 + groups),
        out_specs=ANY,
        out_shape=jax.ShapeDtypeStruct(fine_feats.shape, BF16),
        scratch_shapes=[
            pltpu.VMEM(fine_feats.shape, BF16),
            pltpu.VMEM((padded * SUBS, depth), F32),
            pltpu.VMEM((total * width, voxels // SUBS), BF16),
            pltpu.SemaphoreType.DMA((total // chunk,)),
        ],
        compiler_params=params(28),
        cost_estimate=cost(total * width * voxels * 256, 4 * total * width * voxels),
        name="fine_out",
    )(fine_feats, hidden, empty, lift, weights, spread, *come)


def shards(
    fine_feats, fine_child, parent_block, w_parent, w_root_in, w_root, root_bias, w_down, w_skip
):
    groups = lax.axis_size("ga")
    rows = lax.axis_size("row")
    slots = fine_feats.shape[0]
    padded = -(-slots // META) * META
    pairs = parent_block.shape[0]

    turned, pooled, rest = fine_in(fine_feats, fine_child, parent_block, w_parent, padded)

    hidden = hide(turned, w_parent)
    folded = fold(w_root, w_root_in)

    gathered, others, offsets = [pooled], [rest], [0]
    bit = groups // 2
    while bit:
        swap = [(i, i ^ bit) for i in range(groups)]
        gathered += [lax.ppermute(part, "ga", swap) for part in gathered]
        others += [lax.ppermute(part, "ga", swap) for part in others]
        offsets += [offset ^ bit for offset in offsets]
        if bit == groups // 2:
            others[1], folded, hidden = lax.optimization_barrier((others[1], folded, hidden))
        bit //= 2
    offsets = tuple(offsets)

    faces, table, places, pair, step = place(gathered, others, offsets, folded, padded, pairs)
    pair_swap = [(i, i ^ 1) for i in range(rows) if i ^ 1 < rows]
    step_swap = []
    for i in range(rows):
        inner = 0 < i < rows - 1
        for j in range(groups):
            target = ((i - 1 ^ 1) + 1) * groups + j if inner else i * groups + (j ^ 1)
            step_swap.append((i * groups + j, target))
    pair = lax.ppermute(pair, "row", pair_swap)
    step = lax.ppermute(step, ("row", "ga"), step_swap)
    sums = conv(faces, table, places, folded)
    order = sorted(range(groups), key=lambda k: (offsets[k] > 0, offsets[k] < groups // 2, offsets[k]))
    root, empty, *sends = finish(places, sums, pair, step, root_bias, order, padded)
    come = sends[:1]
    for k, send in zip(order[1:], sends[1:]):
        come.append(lax.ppermute(send, "ga", [(i, i ^ offsets[k]) for i in range(groups)]))
    root_out, lift, weights, spread = unravel(
        root, w_down, w_skip, [offsets[k] for k in order], fine_feats.shape[2]
    )
    fine = fine_out(fine_feats, hidden, empty, lift, weights, spread, come)
    return (fine, root_out)


def solution(mesh):
    return jax.shard_map(
        shards,
        mesh=mesh,
        in_specs=(
            P(("row", "ga"), None, None),
            P(("row", "ga")),
            P(("row", "ga")),
            P(),
            P(),
            P("ga", None, None, None, None),
            P("ga"),
            P(),
            P(),
        ),
        out_specs=(P(("row", "ga"), None, None), P("ga", "row", None, None)),
        check_vma=False,
    )
```
